256 devices in a mesh: band: 4 (over z_hi, core), sx: 4 (over x), sy: 16 (over y, z_lo).
Axes of the slice: x: 4, y: 4, z: 8 (z_hi: 2, z_lo: 4; z = z_hi * 4 + z_lo), core: 2. Of those that a mesh axis runs over, the one named last changes fastest.
Arguments:
- orbitals: float32 [256, 24, 96, 128], P('band', 'sx', 'sy'), may hold values from -6 to 6
- potential: float32 [24, 96, 128], P('sx', 'sy'), may hold values from -3 to 0
- projectors: float32 [256, 4, 5, 128], P(('sx', 'sy')), may hold values from -0.25 to 0.25
- energies: float32 [256, 4], P(('sx', 'sy')), may hold values from 1 to 6
- centers: int32 [256, 2], P(('sx', 'sy')), may hold values from 0 to 95, as said below
Outputs:
- filtered: float32 [256, 24, 96, 128], P('band', 'sx', 'sy')
- gram: float32 [256, 256], P('band')
The draws below stay inside these ranges and needn't reach their ends.
Inputs may be any that keep to these rules, and one draw needn't show every extreme that they name: `centers`: atom a's cell lies in the grid slab of the device numbered a // 4 along sx+sy, sy counting fastest; the first entry indexes the first grid dimension, the second the second.
All inputs are finite; a program needn't handle non-finite values.
Results may differ from the reference program's by a relative error of at most 0.0022.
Values may be sent and summed in bfloat16 or wider, within the bound.
A program may use at most 64 MiB of HBM per device.

```python
import math
import jax
import jax.numpy as jnp
from jax import lax

NB = 256
NPROJ = 4
TPA = 5
NZ = 128
DEG = 2
CX = 6
CY = 6
ATOM_DEV = 4
NX = 24
NY = 96
ATOMS = 256


def draw_orbitals(key, part):
    k_noise, k_base, k_mix = jax.random.split(jax.random.fold_in(key, 3), 3)
    shape = (NB, NX, NY, NZ)
    noise = jax.random.normal(k_noise, shape, jnp.float32)
    base = jax.random.normal(k_base, (NX, NY, NZ), jnp.float32)
    mix = 0.7 * jax.random.normal(k_mix, (NB,), jnp.float32)
    value = mix[:, None, None, None] * base[None] + noise
    return jnp.clip(value, -6.0, 6.0).astype(jnp.float32)


def draw_centers(key, part):
    slabs_y = NY // CY
    count = ATOM_DEV * (NX // CX) * slabs_y
    owner = jnp.arange(count, dtype=jnp.int32) // ATOM_DEV
    index_x = owner // slabs_y
    index_y = owner % slabs_y
    key_x, key_y = jax.random.split(jax.random.fold_in(key, 7), 2)
    cell_x = index_x * CX + jax.random.randint(key_x, (count,), 0, CX, jnp.int32)
    cell_y = index_y * CY + jax.random.randint(key_y, (count,), 0, CY, jnp.int32)
    position = jnp.arange(count, dtype=jnp.int32)
    cell_x = jnp.where(position == 0, 0, cell_x)
    cell_y = jnp.where(position == 0, 0, cell_y)
    cell_x = jnp.where(position == count - 1, NX - 1, cell_x)
    cell_y = jnp.where(position == count - 1, NY - 1, cell_y)
    return jnp.stack([cell_x, cell_y], axis=1).astype(jnp.int32)


def levels(own_key, dims, pieces, smallest, high):
    gain = 1.0
    for dim, blocks in pieces:
        steps = jax.random.uniform(jax.random.fold_in(jax.random.fold_in(own_key, 6), dim), (blocks,), jnp.float32, smallest / len(pieces), high / len(pieces))
        gain = gain * jnp.repeat(jnp.exp(steps), dims[dim] // blocks).reshape((-1,) + (1,) * (len(dims) - 1 - dim))
    return gain


def scatter_about(stream_key, dims, deviation, bound, cuts=(), kind=jnp.bfloat16):
    gain = levels(stream_key, dims, cuts, -0.22, 0.18) if cuts else 1.0
    values = jax.random.normal(stream_key, dims, jnp.float32) * deviation * gain
    return jnp.minimum(jnp.maximum(values, -bound), bound).astype(kind)


def setup_inputs(seed: int = 0) -> dict:
    keys = jax.random.split(jax.random.key(seed), 6)
    return {
        "orbitals": draw_orbitals(jax.random.fold_in(keys[5], 71), 0),
        "potential": jnp.clip(-3.0 + 3.0 * jax.random.uniform(keys[1], (NX, NY, NZ), jnp.float32) ** levels(keys[1], (NX, NY, NZ), ((0, 4), (1, 16)), -0.2, 0.2), -3.0, 0.0),
        "projectors": scatter_about(keys[2], (ATOMS, NPROJ, TPA, NZ), (TPA * NZ) ** -0.5, 0.25, ((0, 64),), jnp.float32),
        "energies": jnp.clip(jnp.exp(math.log(6.0) - 1.7917595 * jax.random.uniform(keys[3], (ATOMS, NPROJ), jnp.float32) ** levels(keys[3], (ATOMS, NPROJ), ((0, 64),), -0.2, 0.2)), 1.0, 6.0),
        "centers": draw_centers(jax.random.fold_in(keys[5], 71), 0),
    }


stencil_weights = (-5369.0 / 1800.0, 12.0 / 7.0, -15.0 / 56.0, 10.0 / 189.0, -1.0 / 112.0, 2.0 / 1925.0, -1.0 / 16632.0)
filter_center = 6.5
filter_half = 6.0
offsets_x = (0, -1, 1, 0, 0)
offsets_y = (0, 0, 0, -1, 1)


def laplace_full(field):
    count_x = field.shape[1]
    count_y = field.shape[2]
    count_z = field.shape[3]
    padded = jnp.pad(field, ((0, 0), (6, 6), (6, 6), (6, 6)))
    total = (3.0 * stencil_weights[0]) * field
    for step in range(1, 7):
        weight = stencil_weights[step]
        total = total + weight * (padded[:, 6 + step:6 + step + count_x, 6:6 + count_y, 6:6 + count_z] + padded[:, 6 - step:6 - step + count_x, 6:6 + count_y, 6:6 + count_z])
        total = total + weight * (padded[:, 6:6 + count_x, 6 + step:6 + step + count_y, 6:6 + count_z] + padded[:, 6:6 + count_x, 6 - step:6 - step + count_y, 6:6 + count_z])
        total = total + weight * (padded[:, 6:6 + count_x, 6:6 + count_y, 6 + step:6 + step + count_z] + padded[:, 6:6 + count_x, 6:6 + count_y, 6 - step:6 - step + count_z])
    return total


def nonlocal_full(field, centers, projectors, energies):
    batch, count_x, count_y, count_z = field.shape
    shift_x = jnp.array(offsets_x, jnp.int32)
    shift_y = jnp.array(offsets_y, jnp.int32)
    cell_x = centers[:, 0:1].astype(jnp.int32) + shift_x[None, :]
    cell_y = centers[:, 1:2].astype(jnp.int32) + shift_y[None, :]
    inside = (cell_x >= 0) & (cell_x < count_x) & (cell_y >= 0) & (cell_y < count_y)
    flat = (jnp.clip(cell_x, 0, count_x - 1) * count_y + jnp.clip(cell_y, 0, count_y - 1)).astype(jnp.int32)
    keep = inside.astype(jnp.float32)
    columns = field.reshape(batch, count_x * count_y, count_z)
    picked = columns[:, flat, :] * keep[None, :, :, None]
    coeffs = jnp.einsum('aptz,batz->bap', projectors, picked, precision=lax.Precision.HIGHEST)
    weighted = coeffs * energies[None]
    spread = jnp.einsum('aptz,bap->batz', projectors, weighted, precision=lax.Precision.HIGHEST) * keep[None, :, :, None]
    result = jnp.zeros_like(columns).at[:, flat.reshape(-1), :].add(spread.reshape(batch, -1, count_z))
    return result.reshape(field.shape)


def reference(orbitals, potential, projectors, energies, centers):
    block = min(16, NB)

    def apply_h(vector):
        return -0.5 * laplace_full(vector) + potential[None] * vector + nonlocal_full(vector, centers, projectors, energies)

    def filter_block(vectors):
        previous = vectors
        current = (apply_h(vectors) - filter_center * vectors) / filter_half
        for degree in range(1, DEG):
            following = 2.0 * (apply_h(current) - filter_center * current) / filter_half - previous
            previous, current = current, following
        return current

    grouped = orbitals.reshape(NB // block, block, NX, NY, NZ)
    filtered = lax.map(filter_block, grouped).reshape(NB, NX, NY, NZ)
    rounded = filtered.astype(jnp.bfloat16).reshape(NB, NX * NY * NZ)
    gram = jnp.dot(rounded, rounded.T, preferred_element_type=jnp.float32) / (NX * NY * NZ)
    return filtered, gram
```

```python
import functools

import jax
import jax.numpy as jnp
from jax import lax
from jax.experimental import pallas as pl
from jax.experimental.pallas import tpu as pltpu
from jax.sharding import PartitionSpec as P

F32 = jnp.float32
BF16 = jnp.bfloat16
MESH = pl.DeviceIdType.MESH

stencil_weights = (
    -5369.0 / 1800.0,
    12.0 / 7.0,
    -15.0 / 56.0,
    10.0 / 189.0,
    -1.0 / 112.0,
    2.0 / 1925.0,
    -1.0 / 16632.0,
)
filter_center = 6.5
filter_half = 6.0

ORB = 64
CHUNKS = 2
ROWS = ORB // CHUNKS
SUB = 16
CELLS = 36
HALF = CELLS // 2
SRC_ROWS = 24
MSG_ROWS = 6 * SRC_ROWS
NT = (((1,), (1,)), ((), ()))
NN = (((1,), (0,)), ((), ()))


def dot(a, b, dims=NN):
    return lax.dot_general(a, b, dims, preferred_element_type=F32)


def split(value):
    high = value.astype(BF16)
    return high, (value - high.astype(F32)).astype(BF16)


def kernel(
    cells_total,
    y0,
    pot,
    proj,
    energies,
    centers,
    out,
    gram,
    y1,
    zn,
    msg,
    weights,
    banded,
    sent,
    halo,
    part,
    part_in,
    coef,
    energy,
    own,
    mate_in,
    far_in,
    cross_in,
    flip,
    flip_in,
    sums,
    scat_in,
    deep,
    deep_in,
    whole,
    s_msg,
    r_msg,
    s_halo,
    r_halo,
    s_part,
    r_part,
    s_coef,
    r_coef,
    s_mate,
    r_mate,
    s_far,
    r_far,
    s_cross,
    r_cross,
    s_flip,
    r_flip,
    s_scat,
    r_scat,
    s_deep,
    r_deep,
    s_whole,
    r_whole,
):
    ix, iy, ib = lax.axis_index("sx"), lax.axis_index("sy"), lax.axis_index("band")
    group, core = ib // 2, lax.rem(ib, 2)
    row_y, low_z = iy // 4, lax.rem(iy, 4)
    plane = ix * 4 + row_y
    near = ({"sx": ix - 1}, {"sx": ix + 1}, {"sy": iy - 1}, {"sy": iy + 1})
    has = (ix > 0, ix < 3, iy > 0, iy < 15)
    mate = {"band": group * 2 + (1 - core)}
    far = {"band": (1 - group) * 2 + core}
    cross = {"band": (1 - group) * 2 + (1 - core)}

    def plane_peer(step):
        other = lax.rem(plane + step, 16)
        return other, {"sx": other // 4, "sy": lax.rem(other, 4) * 4 + low_z}

    def deep_peer(step):
        other = lax.rem(low_z + step, 4)
        return other, {"sy": row_y * 4 + other}

    def remote(src, dst, send, recv, device):
        return pltpu.make_async_remote_copy(
            src_ref=src,
            dst_ref=dst,
            send_sem=send,
            recv_sem=recv,
            device_id=device,
            device_id_type=MESH,
        )

    barrier = pltpu.get_barrier_semaphore()

    def greet(device):
        pl.semaphore_signal(barrier, inc=1, device_id=device, device_id_type=MESH)

    greet({"sx": lax.rem(ix + 1, 4)})
    greet({"sx": lax.rem(ix + 3, 4)})
    greet({"sy": lax.rem(iy + 1, 16)})
    greet({"sy": lax.rem(iy + 15, 16)})
    greet(mate)
    greet(far)
    greet(cross)

    @pl.loop(1, 16)
    def _(step):
        greet(plane_peer(step)[1])

    @pl.loop(1, 4)
    def _(step):
        greet(deep_peer(step)[1])

    line = lax.broadcasted_iota(jnp.int32, (SRC_ROWS, 128), 0)
    atom = line // 5
    tile = line - atom * 5
    shift_x = jnp.where(tile == 1, -1, jnp.where(tile == 2, 1, 0))
    shift_y = jnp.where(tile == 3, -1, jnp.where(tile == 4, 1, 0))
    cell_x = jnp.full((SRC_ROWS, 128), -1000, jnp.int32)
    cell_y = jnp.full((SRC_ROWS, 128), -1000, jnp.int32)
    for a in range(4):
        cell_x = jnp.where(atom == a, centers[a, 0], cell_x)
        cell_y = jnp.where(atom == a, centers[a, 1], cell_y)
    msg[0, 4 * SRC_ROWS : 5 * SRC_ROWS, :] = (cell_x + shift_x).astype(F32)
    msg[0, 5 * SRC_ROWS : 6 * SRC_ROWS, :] = (cell_y + shift_y).astype(F32)
    for p in range(4):
        for a in range(4):
            msg[0, p * SRC_ROWS + 5 * a : p * SRC_ROWS + 5 * a + 5, :] = proj[a, :, p, :]
        msg[0, p * SRC_ROWS + 20 : (p + 1) * SRC_ROWS, :] = jnp.zeros((4, 128), F32)

    pl.semaphore_wait(barrier, 7 + 15 + 3)

    def msg_copy(s):
        return remote(msg.at[0], msg.at[1 + (s ^ 1)], s_msg.at[s], r_msg.at[s ^ 1], near[s])

    def halo_copy(phase, c, s):
        return remote(
            sent.at[phase, c],
            halo.at[phase, c, s ^ 1],
            s_halo.at[phase, c, s],
            r_halo.at[phase, c, s ^ 1],
            near[s],
        )

    def part_copy(phase, c, s):
        return remote(
            part.at[phase, c, 1 + s],
            part_in.at[phase, c, s ^ 1],
            s_part.at[phase, c, s],
            r_part.at[phase, c, s ^ 1],
            near[s],
        )

    def coef_copy(phase, c, s):
        return remote(
            coef.at[phase, c, 0],
            coef.at[phase, c, 1 + (s ^ 1)],
            s_coef.at[phase, c, s],
            r_coef.at[phase, c, s ^ 1],
            near[s],
        )

    def start_all(copy, *index):
        for s in range(4):

            @pl.when(has[s])
            def _(s=s):
                copy(*index, s).start()

    def arrive_all(copy, *index):
        for s in range(4):

            @pl.when(has[s])
            def _(s=s):
                copy(*index, s ^ 1).wait_recv()

    def sent_all(copy, *index):
        for s in range(4):

            @pl.when(has[s])
            def _(s=s):
                copy(*index, s).wait_send()

    start_all(msg_copy)

    def rows_of(c):
        return pl.ds(pl.multiple_of(c * ROWS, ROWS), ROWS)

    def send_first(c):
        for x in range(6):
            sent[0, c, 6 * x : 6 * x + 6] = y0[6 * x : 6 * x + 6, rows_of(c), :].astype(BF16)
        start_all(halo_copy, 0, c)

    send_first(0)

    for s in range(4):

        @pl.when(jnp.logical_not(has[s]))
        def _(s=s):
            msg[1 + s] = jnp.full((MSG_ROWS, 128), -1000.0, F32)
            msg[1 + s, : 4 * SRC_ROWS] = jnp.zeros((4 * SRC_ROWS, 128), F32)
            for phase in range(2):
                for c in range(CHUNKS):
                    halo[phase, c, s] = jnp.zeros((CELLS, ROWS, 128), BF16)
                    part_in[phase, c, s] = jnp.zeros((16, 128), F32)
                    coef[phase, c, 1 + s] = jnp.zeros((16, 128), F32)

    for phase in range(2):
        for c in range(CHUNKS):
            for s in range(5):
                part[phase, c, s] = jnp.zeros((16, 128), F32)

    distance = jnp.abs(
        lax.broadcasted_iota(jnp.int32, (128, 128), 0)
        - lax.broadcasted_iota(jnp.int32, (128, 128), 1)
    )
    band = jnp.zeros((128, 128), F32)
    for step in range(1, 7):
        band = jnp.where(distance == step, -0.5 * stencil_weights[step], band)
    band_high, band_low = split(band)
    banded[0:128, :] = band_high
    banded[128:256, :] = band_high
    banded[256:384, :] = band_low

    slot16 = lax.broadcasted_iota(jnp.int32, (16, 128), 0)
    level = jnp.zeros((16, 128), F32)
    for p in range(4):
        for a in range(4):
            level = jnp.where(slot16 == 4 * p + a, energies[a, p], level)
    energy[...] = level

    arrive_all(msg_copy)
    first_x, first_y = (ix * 6).astype(F32), (iy * 6).astype(F32)
    keys = []
    for s in range(5):
        local_x = msg[s, 4 * SRC_ROWS : 5 * SRC_ROWS, :] - first_x
        local_y = msg[s, 5 * SRC_ROWS : 6 * SRC_ROWS, :] - first_y
        inside = (local_x >= 0) & (local_x < 6) & (local_y >= 0) & (local_y < 6)
        place = (local_x * 6 + local_y) * 80 + (16 * s + atom).astype(F32)
        keys.append(jnp.where(inside & (line < 20), place, -1000.0))
    keys.append(jnp.full((8, 128), -1000.0, F32))
    key = jnp.concatenate(keys, axis=0).T[0:1, :]
    tables = []
    for p in range(4):
        stacked = [msg[s, p * SRC_ROWS : (p + 1) * SRC_ROWS, :] for s in range(5)]
        table = jnp.concatenate(stacked + [jnp.zeros((8, 128), F32)], axis=0)
        tables.append(jnp.concatenate(split(table), axis=1))
    table = jnp.concatenate(tables, axis=0)

    @pl.loop(0, 9)
    def _(block):
        row = lax.broadcasted_iota(jnp.int32, (320, 128), 0) + block * 320
        row = row.astype(F32)
        masks = [
            jnp.where(row == key + 4.0 * p, 1.0, 0.0).astype(BF16) for p in range(4)
        ]
        placed = dot(jnp.concatenate(masks, axis=1), table)
        placed = placed.reshape(4, 80, 256).astype(BF16)
        weights[pl.ds(block * 4, 4), 0:80, :] = placed[:, :, :128]
        weights[pl.ds(block * 4, 4), 80:160, :] = placed[:, :, :128]
        weights[pl.ds(block * 4, 4), 160:240, :] = placed[:, :, 128:]

    def partial(phase, c, source):
        def step(cell, total):
            high, low = split(source(cell))
            w_high, w_low = weights[cell, 0:80, :], weights[cell, 160:240, :]
            left = jnp.concatenate([w_high, w_low, w_high], axis=1)
            right = jnp.concatenate([high, high, low], axis=1)
            return total + dot(left, right, NT)

        total = lax.fori_loop(0, CELLS, step, jnp.zeros((80, ROWS), F32))
        for s in range(5):
            part[phase, c, s, :, 0:ROWS] = total[16 * s : 16 * s + 16, :]
        start_all(part_copy, phase, c)

    def finish_coef(phase, c):
        arrive_all(part_copy, phase, c)
        total = part[phase, c, 0]
        for s in range(4):
            total = total + part_in[phase, c, s]
        coef[phase, c, 0] = total * energy[...]
        start_all(coef_copy, phase, c)

    def along_z(source):
        for x in range(6):
            high, low = split(source(x).reshape(6 * ROWS, 128))
            left = jnp.concatenate([high, low, high], axis=1)
            zn[6 * x : 6 * x + 6] = dot(left, banded[...]).reshape(6, ROWS, 128)

    def projected(phase, c):
        arrive_all(coef_copy, phase, c)
        stacked = jnp.concatenate([coef[phase, c, s] for s in range(5)], axis=0)
        high = stacked.astype(BF16).astype(F32)
        low = (stacked - high).astype(BF16).astype(F32)
        left = jnp.concatenate([high, low, high], axis=0).T[0:ROWS, :].astype(BF16)

        @pl.loop(0, CELLS)
        def _(cell):
            zn[cell] += dot(left, weights[cell])

    center = -1.5 * stencil_weights[0] - filter_center

    def stencil(phase, c, source, finish):
        @pl.loop(0, ROWS // SUB)
        def _(block):
            rows = pl.ds(pl.multiple_of(block * SUB, SUB), SUB)
            for x in range(6):

                def layer(other):
                    if other < 0:
                        return halo[phase, c, 0, 6 * (other + 6) : 6 * (other + 7), rows, :].astype(F32)
                    if other > 5:
                        return halo[phase, c, 1, 6 * (other - 6) : 6 * (other - 5), rows, :].astype(F32)
                    return source(other, block)

                here = source(x, block)
                line_y = jnp.concatenate(
                    [
                        halo[phase, c, 2, 6 * x : 6 * x + 6, rows, :].astype(F32),
                        here,
                        halo[phase, c, 3, 6 * x : 6 * x + 6, rows, :].astype(F32),
                    ],
                    axis=0,
                )
                total = zn[6 * x : 6 * x + 6, rows, :]
                total = total + here * (pot[x][:, None, :] + center)
                for step in range(1, 7):
                    weight = -0.5 * stencil_weights[step]
                    pair = layer(x - step) + layer(x + step)
                    pair = pair + line_y[6 - step : 12 - step] + line_y[6 + step : 12 + step]
                    total = total + weight * pair
                finish(x, block, total)

    def block_rows(c, block):
        return pl.ds(pl.multiple_of(c * ROWS + block * SUB, SUB), SUB)

    for c in range(CHUNKS):
        partial(0, c, lambda cell, c=c: y0[cell, rows_of(c), :])
    for c in range(1, CHUNKS):
        send_first(c)
    for c in range(CHUNKS):
        finish_coef(0, c)

    @pl.loop(0, CHUNKS)
    def _(c):
        along_z(lambda x: y0[6 * x : 6 * x + 6, rows_of(c), :])
        projected(0, c)
        arrive_all(halo_copy, 0, c)

        def finish(x, block, total):
            value = total * (1.0 / filter_half)
            y1[c, 6 * x : 6 * x + 6, pl.ds(pl.multiple_of(block * SUB, SUB), SUB), :] = value
            sent[1, c, 6 * x : 6 * x + 6, pl.ds(pl.multiple_of(block * SUB, SUB), SUB), :] = (
                value.astype(BF16)
            )

        stencil(
            0, c, lambda x, block: y0[6 * x : 6 * x + 6, block_rows(c, block), :], finish
        )
        start_all(halo_copy, 1, c)
        partial(1, c, lambda cell: y1[c, cell])

    @pl.loop(0, CHUNKS)
    def _(c):
        finish_coef(1, c)

    def mate_copy(c):
        return remote(own.at[c], mate_in.at[c], s_mate.at[c], r_mate.at[c], mate)

    def far_copy(c):
        start = pl.multiple_of(group * HALF, HALF)
        return remote(
            own.at[c, pl.ds(start, HALF)], far_in.at[c], s_far.at[c], r_far.at[c], far
        )

    def cross_copy(c):
        return remote(far_in.at[c], cross_in.at[c], s_cross.at[c], r_cross.at[c], mate)

    @pl.loop(0, CHUNKS)
    def _(c):
        along_z(lambda x: y1[c, 6 * x : 6 * x + 6])
        projected(1, c)
        arrive_all(halo_copy, 1, c)

        def finish(x, block, total):
            before = y0[6 * x : 6 * x + 6, block_rows(c, block), :]
            value = total * (2.0 / filter_half) - before
            out[6 * x : 6 * x + 6, block_rows(c, block), :] = value
            own[c, 6 * x : 6 * x + 6, pl.ds(pl.multiple_of(block * SUB, SUB), SUB), :] = (
                value.astype(BF16)
            )

        stencil(
            1,
            c,
            lambda x, block: y1[
                c, 6 * x : 6 * x + 6, pl.ds(pl.multiple_of(block * SUB, SUB), SUB), :
            ],
            finish,
        )
        far_copy(c).start()
        mate_copy(c).start()

    @pl.loop(0, CHUNKS)
    def _(c):
        far_copy(c).wait_recv()
        cross_copy(c).start()

    @pl.loop(0, CHUNKS)
    def _(c):
        mate_copy(c).wait_recv()

    def gather(ref, cell):
        return jnp.concatenate([ref[c, cell] for c in range(CHUNKS)], axis=0)

    def in_order(first, second):
        return jnp.concatenate(
            [jnp.where(core == 0, first, second), jnp.where(core == 0, second, first)], axis=0
        )

    def near_step(cell, total):
        mine = gather(own, cell)
        return total + dot(mine, in_order(mine, gather(mate_in, cell)), NT)

    near_sum = lax.fori_loop(0, CELLS, near_step, jnp.zeros((ORB, 128), F32))

    @pl.loop(0, CHUNKS)
    def _(c):
        cross_copy(c).wait_recv()

    def far_step(cell, totals):
        mine = gather(own, (1 - group) * HALF + cell)
        theirs, others = gather(far_in, cell), gather(cross_in, cell)
        straight = totals[0] + dot(mine, in_order(theirs, others), NT)
        both = jnp.concatenate([theirs, others], axis=0)
        zero = jnp.zeros_like(mine)
        turned = totals[1] + dot(both, in_order(mine, zero), NT)
        return straight, turned

    far_sum, turned = lax.fori_loop(
        0, HALF, far_step, (jnp.zeros((ORB, 128), F32), jnp.zeros((2 * ORB, 128), F32))
    )
    flip[0] = turned[:ORB]
    flip[1] = turned[ORB:]
    flip_far = remote(flip.at[0], flip_in.at[0], s_flip.at[0], r_flip.at[0], far)
    flip_cross = remote(flip.at[1], flip_in.at[1], s_flip.at[1], r_flip.at[1], cross)
    flip_far.start()
    flip_cross.start()
    sums[0:ORB] = near_sum
    flip_far.wait_recv()
    flip_cross.wait_recv()
    sums[ORB : 2 * ORB] = far_sum + flip_in[0] + flip_in[1]

    def scat_copy(step):
        other, device = plane_peer(step)
        start = pl.multiple_of(other * 8, 8)
        return remote(
            sums.at[pl.ds(start, 8)], scat_in.at[step], s_scat.at[step], r_scat.at[step], device
        )

    def whole_copy(step):
        other, device = plane_peer(step)
        start = pl.multiple_of(plane * 8, 8)
        return remote(
            whole.at[pl.ds(start, 8)],
            whole.at[pl.ds(start, 8)],
            s_whole.at[step],
            r_whole.at[step],
            device,
        )

    def deep_copy(step):
        other, device = deep_peer(step)
        return remote(deep, deep_in.at[step], s_deep.at[step], r_deep.at[step], device)

    @pl.loop(1, 16)
    def _(step):
        scat_copy(step).start()

    def add_scat(step, total):
        scat_copy(step).wait_recv()
        return total + scat_in[step]

    mine = sums[pl.ds(pl.multiple_of(plane * 8, 8), 8), :]
    mine = lax.fori_loop(1, 16, add_scat, mine)
    deep[...] = mine
    for step in range(1, 4):
        deep_copy(step).start()
    for step in range(1, 4):
        deep_copy(step).wait_recv()
        mine = mine + deep_in[step]
    whole[pl.ds(pl.multiple_of(plane * 8, 8), 8), :] = mine * (1.0 / cells_total)

    @pl.loop(1, 16)
    def _(step):
        whole_copy(step).start()

    @pl.loop(1, 16)
    def _(step):
        other = lax.rem(plane + 16 - step, 16)
        start = pl.multiple_of(other * 8, 8)
        remote(
            whole.at[pl.ds(start, 8)],
            whole.at[pl.ds(start, 8)],
            s_whole.at[step],
            r_whole.at[step],
            plane_peer(step)[1],
        ).wait_recv()

    near_all, far_all = whole[0:ORB, :], whole[ORB : 2 * ORB, :]
    gram[:, 0:128] = jnp.where(group == 0, near_all, far_all)
    gram[:, 128:256] = jnp.where(group == 0, far_all, near_all)

    sent_all(msg_copy)
    for phase in range(2):

        @pl.loop(0, CHUNKS)
        def _(c, phase=phase):
            sent_all(halo_copy, phase, c)
            sent_all(part_copy, phase, c)
            sent_all(coef_copy, phase, c)

    @pl.loop(0, CHUNKS)
    def _(c):
        mate_copy(c).wait_send()
        far_copy(c).wait_send()
        cross_copy(c).wait_send()

    flip_far.wait_send()
    flip_cross.wait_send()

    @pl.loop(1, 16)
    def _(step):
        scat_copy(step).wait_send()
        whole_copy(step).wait_send()

    for step in range(1, 4):
        deep_copy(step).wait_send()


def local(orbitals, potential, projectors, energies, centers):
    y0 = orbitals.transpose(1, 2, 0, 3).reshape(CELLS, ORB, 128)
    proj = projectors.transpose(0, 2, 1, 3)
    cells_total = CELLS * 128 * lax.axis_size("sx") * lax.axis_size("sy")
    vmem = pl.BlockSpec(memory_space=pltpu.VMEM)
    smem = pl.BlockSpec(memory_space=pltpu.SMEM)
    dma = pltpu.SemaphoreType.DMA
    chunk = (CHUNKS, CELLS, ROWS, 128)
    half = (CHUNKS, HALF, ROWS, 128)
    out, gram = pl.pallas_call(
        functools.partial(kernel, cells_total),
        out_shape=(
            jax.ShapeDtypeStruct((CELLS, ORB, 128), F32),
            jax.ShapeDtypeStruct((ORB, 256), F32),
        ),
        in_specs=[vmem, vmem, vmem, smem, smem],
        out_specs=(vmem, vmem),
        scratch_shapes=[
            pltpu.VMEM(chunk, F32),
            pltpu.VMEM((CELLS, ROWS, 128), F32),
            pltpu.VMEM((5, MSG_ROWS, 128), F32),
            pltpu.VMEM((CELLS, 240, 128), BF16),
            pltpu.VMEM((384, 128), BF16),
            pltpu.VMEM((2,) + chunk, BF16),
            pltpu.VMEM((2, CHUNKS, 4, CELLS, ROWS, 128), BF16),
            pltpu.VMEM((2, CHUNKS, 5, 16, 128), F32),
            pltpu.VMEM((2, CHUNKS, 4, 16, 128), F32),
            pltpu.VMEM((2, CHUNKS, 5, 16, 128), F32),
            pltpu.VMEM((16, 128), F32),
            pltpu.VMEM(chunk, BF16),
            pltpu.VMEM(chunk, BF16),
            pltpu.VMEM(half, BF16),
            pltpu.VMEM(half, BF16),
            pltpu.VMEM((2, ORB, 128), F32),
            pltpu.VMEM((2, ORB, 128), F32),
            pltpu.VMEM((2 * ORB, 128), F32),
            pltpu.VMEM((16, 8, 128), F32),
            pltpu.VMEM((8, 128), F32),
            pltpu.VMEM((4, 8, 128), F32),
            pltpu.VMEM((2 * ORB, 128), F32),
            dma((4,)),
            dma((4,)),
            dma((2, CHUNKS, 4)),
            dma((2, CHUNKS, 4)),
            dma((2, CHUNKS, 4)),
            dma((2, CHUNKS, 4)),
            dma((2, CHUNKS, 4)),
            dma((2, CHUNKS, 4)),
            dma((CHUNKS,)),
            dma((CHUNKS,)),
            dma((CHUNKS,)),
            dma((CHUNKS,)),
            dma((CHUNKS,)),
            dma((CHUNKS,)),
            dma((2,)),
            dma((2,)),
            dma((16,)),
            dma((16,)),
            dma((4,)),
            dma((4,)),
            dma((16,)),
            dma((16,)),
        ],
        compiler_params=pltpu.CompilerParams(
            collective_id=0, has_side_effects=True, vmem_limit_bytes=48 * 1024 * 1024
        ),
        name="filter_and_gram",
    )(y0, potential, proj, energies, centers)
    filtered = out.reshape(6, 6, ORB, 128).transpose(2, 0, 1, 3)
    return filtered, gram


def solution(mesh):
    in_specs = (
        P("band", "sx", "sy", None),
        P("sx", "sy", None),
        P(("sx", "sy"), None, None, None),
        P(("sx", "sy"), None),
        P(("sx", "sy"), None),
    )
    out_specs = (P("band", "sx", "sy", None), P("band", None))
    return jax.shard_map(local, mesh=mesh, in_specs=in_specs, out_specs=out_specs, check_vma=False)
```

```python
import functools

import jax
import jax.numpy as jnp
from jax import lax
from jax.experimental import pallas as pl
from jax.experimental.pallas import tpu as pltpu
from jax.sharding import PartitionSpec as P

F32 = jnp.float32
BF16 = jnp.bfloat16
MESH = pl.DeviceIdType.MESH

stencil_weights = (
    -5369.0 / 1800.0,
    12.0 / 7.0,
    -15.0 / 56.0,
    10.0 / 189.0,
    -1.0 / 112.0,
    2.0 / 1925.0,
    -1.0 / 16632.0,
)
filter_center = 6.5
filter_half = 6.0

ORB = 64
CHUNKS = 4
ROWS = ORB // CHUNKS
CELLS = 36
HALF = CELLS // 2
PAIRS = 20
MSG_ROWS = 4 * PAIRS + 8
GROUP = ORB // 2
NT = (((1,), (1,)), ((), ()))
NN = (((1,), (0,)), ((), ()))


def dot(a, b, dims=NN):
    return lax.dot_general(a, b, dims, preferred_element_type=F32)


def split(value):
    high = value.astype(BF16)
    return high, (value - high.astype(F32)).astype(BF16)


def kernel(
    cells_total,
    y0_hbm,
    pot_hbm,
    proj_hbm,
    energies,
    centers,
    out,
    gram,
    y0,
    pot,
    proj,
    y1,
    zn,
    msg,
    weights,
    banded,
    sent,
    halo,
    part,
    part_in,
    coef,
    energy,
    wide,
    own,
    mate_in,
    far_in,
    cross_in,
    sums,
    scat_in,
    deep,
    deep_in,
    turn_in,
    whole,
    s_load,
    s_msg,
    r_msg,
    s_halo,
    r_halo,
    s_part,
    r_part,
    s_coef,
    r_coef,
    s_mate,
    r_mate,
    s_far,
    r_far,
    s_cross,
    r_cross,
    s_scat,
    r_scat,
    s_deep,
    r_deep,
    s_turn,
    r_turn,
    s_whole,
    r_whole,
):
    ix, iy, ib = lax.axis_index("sx"), lax.axis_index("sy"), lax.axis_index("band")
    group, core = ib // 2, lax.rem(ib, 2)
    row_y, low_z = iy // 4, lax.rem(iy, 4)
    plane = ix * 4 + row_y
    near = ({"sx": ix - 1}, {"sx": ix + 1}, {"sy": iy - 1}, {"sy": iy + 1})
    has = (ix > 0, ix < 3, iy > 0, iy < 15)
    mate = {"band": group * 2 + (1 - core)}
    far = {"band": (1 - group) * 2 + core}
    cross = {"band": (1 - group) * 2 + (1 - core)}

    def plane_peer(step):
        other = lax.rem(plane + step, 16)
        return other, {"sx": other // 4, "sy": lax.rem(other, 4) * 4 + low_z}

    def deep_peer(step):
        other = lax.rem(low_z + step, 4)
        return other, {"sy": row_y * 4 + other}

    def remote(src, dst, send, recv, device):
        return pltpu.make_async_remote_copy(
            src_ref=src,
            dst_ref=dst,
            send_sem=send,
            recv_sem=recv,
            device_id=device,
            device_id_type=MESH,
        )

    loads = [
        pltpu.make_async_copy(proj_hbm, proj, s_load.at[0]),
        pltpu.make_async_copy(y0_hbm, y0, s_load.at[1]),
        pltpu.make_async_copy(pot_hbm, pot, s_load.at[2]),
    ]
    for load in loads:
        load.start()
    barrier = pltpu.get_barrier_semaphore()

    def greet(device):
        pl.semaphore_signal(barrier, inc=1, device_id=device, device_id_type=MESH)

    greet({"sx": lax.rem(ix + 1, 4)})
    greet({"sx": lax.rem(ix + 3, 4)})
    greet({"sy": lax.rem(iy + 1, 16)})
    greet({"sy": lax.rem(iy + 15, 16)})
    greet(mate)
    greet(far)
    greet(cross)

    @pl.loop(1, 16)
    def _(step):
        greet(plane_peer(step)[1])

    @pl.loop(1, 4)
    def _(step):
        device = deep_peer(step)[1]
        greet(device)
        greet({**device, **far})
        greet({**device, **cross})

    lane = lax.broadcasted_iota(jnp.int32, (8, 128), 1)
    atom = lane // 5
    tile = lane - atom * 5
    shift_x = jnp.where(tile == 1, -1, jnp.where(tile == 2, 1, 0))
    shift_y = jnp.where(tile == 3, -1, jnp.where(tile == 4, 1, 0))
    cell_x = jnp.full((8, 128), -1000, jnp.int32)
    cell_y = jnp.full((8, 128), -1000, jnp.int32)
    for a in range(4):
        cell_x = jnp.where(atom == a, centers[0, a], cell_x)
        cell_y = jnp.where(atom == a, centers[1, a], cell_y)
    line = lax.broadcasted_iota(jnp.int32, (8, 128), 0)
    cells = jnp.where(line == 0, cell_x + shift_x, cell_y + shift_y)
    msg[0, 4 * PAIRS : MSG_ROWS, :] = cells.astype(F32)
    loads[0].wait()
    for p in range(4):
        for a in range(4):
            start = p * PAIRS + 5 * a
            msg[0, start : start + 5, :] = proj[a, :, p, :]

    for s in range(4):

        @pl.when(jnp.logical_not(has[s]))
        def _(s=s):
            msg[1 + s] = jnp.zeros((MSG_ROWS, 128), F32)
            msg[1 + s, 4 * PAIRS : MSG_ROWS] = jnp.full((8, 128), -1000.0, F32)
            for phase in range(2):
                for c in range(CHUNKS):
                    halo[phase, c, s] = jnp.zeros((CELLS, ROWS, 128), BF16)
            for k in range(3):
                part_in[k, s] = jnp.zeros((8, 128), F32)
                coef[k, 1 + s] = jnp.zeros((8, 128), F32)

    wide[...] = jnp.zeros((80, 128), F32)

    distance = jnp.abs(
        lax.broadcasted_iota(jnp.int32, (128, 128), 0)
        - lax.broadcasted_iota(jnp.int32, (128, 128), 1)
    )
    band = jnp.zeros((128, 128), F32)
    for step in range(1, 7):
        band = jnp.where(distance == step, -0.5 * stencil_weights[step], band)
    band_high, band_low = split(band)
    banded[0:128, :] = band_high
    banded[128:256, :] = band_high
    banded[256:384, :] = band_low

    level = jnp.zeros((8, 128), F32)
    for p in range(4):
        for a in range(4):
            row = 4 * p + a
            here = (line == row % 8) & ((lane >= 64) == (row >= 8))
            level = jnp.where(here, energies[a, p], level)
    energy[...] = level

    def rows_of(c):
        return pl.ds(pl.multiple_of(c * ROWS, ROWS), ROWS)

    loads[1].wait()
    for c in range(CHUNKS):
        for x in range(6):
            sent[0, c, 6 * x : 6 * x + 6] = y0[6 * x : 6 * x + 6, rows_of(c), :].astype(BF16)

    pl.semaphore_wait(barrier, 7 + 15 + 9)

    def msg_copy(s):
        return remote(msg.at[0], msg.at[1 + (s ^ 1)], s_msg.at[s], r_msg.at[s ^ 1], near[s])

    def halo_copy(phase, c, s):
        return remote(
            sent.at[phase, c],
            halo.at[phase, c, s ^ 1],
            s_halo.at[phase, c, s],
            r_halo.at[phase, c, s ^ 1],
            near[s],
        )

    def part_copy(k, s):
        return remote(
            part.at[k, 1 + s], part_in.at[k, s ^ 1], s_part.at[k, s], r_part.at[k, s ^ 1], near[s]
        )

    def coef_copy(k, s):
        return remote(
            coef.at[k, 0], coef.at[k, 1 + (s ^ 1)], s_coef.at[k, s], r_coef.at[k, s ^ 1], near[s]
        )

    def start_all(copy, *index):
        for s in range(4):

            @pl.when(has[s])
            def _(s=s):
                copy(*index, s).start()

    def arrive_all(copy, *index):
        for s in range(4):

            @pl.when(has[s])
            def _(s=s):
                copy(*index, s ^ 1).wait_recv()

    def sent_all(copy, *index):
        for s in range(4):

            @pl.when(has[s])
            def _(s=s):
                copy(*index, s).wait_send()

    start_all(msg_copy)
    start_all(halo_copy, 0, 0)

    arrive_all(msg_copy)
    first_x, first_y = (ix * 6).astype(F32), (iy * 6).astype(F32)
    key = jnp.full((1, 128), -1000.0, F32)
    wide_atom = atom.astype(F32)
    for s in range(5):
        coords = msg[s, 4 * PAIRS : MSG_ROWS, :]
        local_x, local_y = coords[0:1] - first_x, coords[1:2] - first_y
        inside = (local_x >= 0) & (local_x < 6) & (local_y >= 0) & (local_y < 6)
        inside = inside & (lane[0:1] < PAIRS)
        place = (local_x * 6 + local_y) * 80 + (16.0 * s + wide_atom[0:1])
        place = jnp.broadcast_to(jnp.where(inside, place, -1000.0), (8, 128))
        moved = pltpu.roll(place, PAIRS * s, 1)[0:1] if s else place[0:1]
        mine = (lane[0:1] >= PAIRS * s) & (lane[0:1] < PAIRS * (s + 1))
        key = jnp.where(mine, moved, key)
    tables = []
    for p in range(4):
        stacked = [msg[s, p * PAIRS : (p + 1) * PAIRS, :] for s in range(5)]
        table = jnp.concatenate(stacked + [jnp.zeros((28, 128), F32)], axis=0)
        tables.append(jnp.concatenate(split(table), axis=1))
    table = jnp.concatenate(tables, axis=0)

    @pl.loop(0, 9, unroll=3)
    def _(block):
        row = lax.broadcasted_iota(jnp.int32, (320, 128), 0) + block * 320
        row = row.astype(F32)
        masks = [
            jnp.where(row == key + 4.0 * p, 1.0, 0.0).astype(BF16) for p in range(4)
        ]
        placed = dot(jnp.concatenate(masks, axis=1), table)
        placed = placed.reshape(4, 80, 256).astype(BF16)
        weights[pl.ds(block * 4, 4), 0:80, :] = placed[:, :, :128]
        weights[pl.ds(block * 4, 4), 80:160, :] = placed[:, :, :128]
        weights[pl.ds(block * 4, 4), 160:240, :] = placed[:, :, 128:]

    def partial(k, count, source):
        def step(cell, total):
            high, low = split(source(cell))
            w_high, w_low = weights[cell, 0:80, :], weights[cell, 160:240, :]
            left = jnp.concatenate([w_high, w_low, w_high], axis=1)
            right = jnp.concatenate([high, high, low], axis=1)
            return total + dot(left, right, NT)

        total = lax.fori_loop(0, CELLS, step, jnp.zeros((80, count), F32), unroll=12)
        wide[:, 0:count] = total
        for s in range(5):
            upper = pltpu.roll(wide[16 * s + 8 : 16 * s + 16, :], 64, 1)
            part[k, s] = jnp.where(lane < 64, wide[16 * s : 16 * s + 8, :], upper)
        start_all(part_copy, k)

    def finish_coef(k):
        arrive_all(part_copy, k)
        total = part[k, 0]
        for s in range(4):
            total = total + part_in[k, s]
        coef[k, 0] = total * energy[...]
        start_all(coef_copy, k)

    def along_z(rows, count, source):
        for x in range(6):
            high, low = split(source(x).reshape(6 * count, 128))
            left = jnp.concatenate([high, low, high], axis=1)
            zn[6 * x : 6 * x + 6, rows] = dot(left, banded[...]).reshape(6, count, 128)

    def projected(k, rows, count):
        arrive_all(coef_copy, k)
        parts = []
        for s in range(5):
            parts += [coef[k, s], pltpu.roll(coef[k, s], 64, 1)]
        stacked = jnp.concatenate(parts, axis=0)
        high = stacked.astype(BF16).astype(F32)
        low = (stacked - high).astype(BF16).astype(F32)
        left = jnp.concatenate([high, low, high], axis=0).T[0:count, :].astype(BF16)

        @pl.loop(0, CELLS, unroll=12)
        def _(cell):
            zn[cell, rows] += dot(left, weights[cell])

    center = -1.5 * stencil_weights[0] - filter_center

    def stencil(phase, c, source, finish):
        for x in range(6):

            def layer(other):
                if other < 0:
                    return halo[phase, c, 0, 6 * (other + 6) : 6 * (other + 7)].astype(F32)
                if other > 5:
                    return halo[phase, c, 1, 6 * (other - 6) : 6 * (other - 5)].astype(F32)
                return source(other)

            here = source(x)
            line_y = jnp.concatenate(
                [
                    halo[phase, c, 2, 6 * x : 6 * x + 6].astype(F32),
                    here,
                    halo[phase, c, 3, 6 * x : 6 * x + 6].astype(F32),
                ],
                axis=0,
            )
            total = zn[6 * x : 6 * x + 6, rows_of(c), :]
            total = total + here * (pot[x][:, None, :] + center)
            for step in range(1, 7):
                weight = -0.5 * stencil_weights[step]
                pair = layer(x - step) + layer(x + step)
                pair = pair + line_y[6 - step : 12 - step] + line_y[6 + step : 12 + step]
                total = total + weight * pair
            finish(x, total)

    everyone = pl.ds(0, ORB)
    partial(0, ORB, lambda cell: y0[cell])
    start_all(halo_copy, 0, 1)
    finish_coef(0)
    start_all(halo_copy, 0, 2)
    start_all(halo_copy, 0, 3)
    along_z(everyone, ORB, lambda x: y0[6 * x : 6 * x + 6])
    loads[2].wait()
    projected(0, everyone, ORB)

    def group_rows(g):
        return pl.ds(pl.multiple_of(g * GROUP, GROUP), GROUP)

    @pl.loop(0, 2)
    def _(g):
        @pl.loop(2 * g, 2 * g + 2)
        def _(c):
            arrive_all(halo_copy, 0, c)

            def finish(x, total):
                value = total * (1.0 / filter_half)
                y1[6 * x : 6 * x + 6, rows_of(c), :] = value
                sent[1, c, 6 * x : 6 * x + 6] = value.astype(BF16)

            stencil(0, c, lambda x: y0[6 * x : 6 * x + 6, rows_of(c), :], finish)

        partial(1 + g, GROUP, lambda cell: y1[cell, group_rows(g), :])
        start_all(halo_copy, 1, g)

    finish_coef(1)
    finish_coef(2)
    start_all(halo_copy, 1, 2)
    start_all(halo_copy, 1, 3)

    def mate_copy(c):
        return remote(own.at[c], mate_in.at[c], s_mate.at[c], r_mate.at[c], mate)

    def far_copy(c):
        start = pl.multiple_of(group * HALF, HALF)
        return remote(
            own.at[c, pl.ds(start, HALF)], far_in.at[c], s_far.at[c], r_far.at[c], far
        )

    def cross_copy(c):
        return remote(far_in.at[c], cross_in.at[c], s_cross.at[c], r_cross.at[c], mate)

    @pl.loop(0, 2)
    def _(g):
        along_z(group_rows(g), GROUP, lambda x: y1[6 * x : 6 * x + 6, group_rows(g), :])
        projected(1 + g, group_rows(g), GROUP)

        @pl.loop(2 * g, 2 * g + 2)
        def _(c):
            arrive_all(halo_copy, 1, c)

            def finish(x, total):
                before = y0[6 * x : 6 * x + 6, rows_of(c), :]
                value = total * (2.0 / filter_half) - before
                out[6 * x : 6 * x + 6, rows_of(c), :] = value
                own[c, 6 * x : 6 * x + 6] = value.astype(BF16)

            stencil(1, c, lambda x: y1[6 * x : 6 * x + 6, rows_of(c), :], finish)
            far_copy(c).start()
            mate_copy(c).start()

    @pl.loop(0, CHUNKS)
    def _(c):
        far_copy(c).wait_recv()
        cross_copy(c).start()

    @pl.loop(0, CHUNKS)
    def _(c):
        mate_copy(c).wait_recv()

    def gather(ref, cell):
        return jnp.concatenate([ref[c, cell] for c in range(CHUNKS)], axis=0)

    def in_order(first, second):
        return jnp.concatenate(
            [jnp.where(core == 0, first, second), jnp.where(core == 0, second, first)], axis=0
        )

    def near_step(cell, total):
        mine = gather(own, cell)
        return total + dot(mine, in_order(mine, gather(mate_in, cell)), NT)

    near_sum = lax.fori_loop(0, CELLS, near_step, jnp.zeros((ORB, 128), F32), unroll=12)

    @pl.loop(0, CHUNKS)
    def _(c):
        cross_copy(c).wait_recv()

    def far_step(cell, totals):
        mine = gather(own, (1 - group) * HALF + cell)
        theirs, others = gather(far_in, cell), gather(cross_in, cell)
        straight = totals[0] + dot(mine, in_order(theirs, others), NT)
        both = jnp.concatenate([theirs, others], axis=0)
        zero = jnp.zeros_like(mine)
        turned = totals[1] + dot(both, in_order(mine, zero), NT)
        return straight, turned

    start = (jnp.zeros((ORB, 128), F32), jnp.zeros((2 * ORB, 128), F32))
    far_sum, turned = lax.fori_loop(0, HALF, far_step, start, unroll=9)

    for q in range(16):
        rows = slice(4 * q, 4 * q + 4)
        sums[q, 0:4] = near_sum[rows]
        sums[q, 4:8] = far_sum[rows]
        sums[q, 8:12] = turned[rows]
        sums[q, 12:16] = turned[ORB + 4 * q : ORB + 4 * q + 4]

    def scat_copy(step):
        other, device = plane_peer(step)
        return remote(
            sums.at[other], scat_in.at[step], s_scat.at[step], r_scat.at[step], device
        )

    def whole_copy(step):
        device = plane_peer(step)[1]
        return remote(
            whole.at[plane], whole.at[plane], s_whole.at[step], r_whole.at[step], device
        )

    def deep_copy(step):
        device = deep_peer(step)[1]
        return remote(deep.at[0], deep_in.at[step], s_deep.at[step], r_deep.at[step], device)

    def turn_copy(side, step):
        device = {**deep_peer(step)[1], **(far, cross)[side]}
        return remote(
            deep.at[1],
            turn_in.at[side, step],
            s_turn.at[side, step],
            r_turn.at[side, step],
            device,
        )

    @pl.loop(1, 16)
    def _(step):
        scat_copy(step).start()

    def add_scat(step, total):
        scat_copy(step).wait_recv()
        return total + scat_in[step]

    mine = lax.fori_loop(1, 16, add_scat, sums[plane])
    deep[0] = mine[0:8]
    deep[1] = mine[8:16]
    for step in range(4):
        for side in range(2):
            turn_copy(side, step).start()
    for step in range(1, 4):
        deep_copy(step).start()
    mine = mine[0:8]
    for step in range(1, 4):
        deep_copy(step).wait_recv()
        mine = mine + deep_in[step]
    turned_in = jnp.zeros((4, 128), F32)
    for step in range(4):
        for side in range(2):
            turn_copy(side, step).wait_recv()
            turned_in = turned_in + turn_in[side, step, 4 * side : 4 * side + 4]
    mine = mine + jnp.concatenate([jnp.zeros((4, 128), F32), turned_in], axis=0)
    whole[plane] = mine * (1.0 / cells_total)

    @pl.loop(1, 16)
    def _(step):
        whole_copy(step).start()

    @pl.loop(1, 16)
    def _(step):
        other = lax.rem(plane + 16 - step, 16)
        remote(
            whole.at[other],
            whole.at[other],
            s_whole.at[step],
            r_whole.at[step],
            plane_peer(step)[1],
        ).wait_recv()

    for q in range(16):
        near_rows, far_rows = whole[q, 0:4], whole[q, 4:8]
        gram[4 * q : 4 * q + 4, 0:128] = jnp.where(group == 0, near_rows, far_rows)
        gram[4 * q : 4 * q + 4, 128:256] = jnp.where(group == 0, far_rows, near_rows)

    sent_all(msg_copy)
    for phase in range(2):

        @pl.loop(0, CHUNKS)
        def _(c, phase=phase):
            sent_all(halo_copy, phase, c)

    @pl.loop(0, 3)
    def _(k):
        sent_all(part_copy, k)
        sent_all(coef_copy, k)

    @pl.loop(0, CHUNKS)
    def _(c):
        mate_copy(c).wait_send()
        far_copy(c).wait_send()
        cross_copy(c).wait_send()

    @pl.loop(1, 16)
    def _(step):
        scat_copy(step).wait_send()
        whole_copy(step).wait_send()

    for step in range(4):
        for side in range(2):
            turn_copy(side, step).wait_send()
    for step in range(1, 4):
        deep_copy(step).wait_send()


def local(orbitals, potential, projectors, energies, centers):
    y0 = orbitals.transpose(1, 2, 0, 3).reshape(CELLS, ORB, 128)
    proj = projectors.transpose(0, 2, 1, 3)
    cells_total = CELLS * 128 * lax.axis_size("sx") * lax.axis_size("sy")
    vmem = pl.BlockSpec(memory_space=pltpu.VMEM)
    anywhere = pl.BlockSpec(memory_space=pl.ANY)
    smem = pl.BlockSpec(memory_space=pltpu.SMEM)
    dma = pltpu.SemaphoreType.DMA
    chunk = (CHUNKS, CELLS, ROWS, 128)
    half = (CHUNKS, HALF, ROWS, 128)
    out, gram = pl.pallas_call(
        functools.partial(kernel, cells_total),
        out_shape=(
            jax.ShapeDtypeStruct((CELLS, ORB, 128), F32),
            jax.ShapeDtypeStruct((ORB, 256), F32),
        ),
        in_specs=[anywhere, anywhere, anywhere, smem, smem],
        out_specs=(vmem, vmem),
        scratch_shapes=[
            pltpu.VMEM((CELLS, ORB, 128), F32),
            pltpu.VMEM((6, 6, 128), F32),
            pltpu.VMEM((4, 5, 4, 128), F32),
            pltpu.VMEM((CELLS, ORB, 128), F32),
            pltpu.VMEM((CELLS, ORB, 128), F32),
            pltpu.VMEM((5, MSG_ROWS, 128), F32),
            pltpu.VMEM((CELLS, 240, 128), BF16),
            pltpu.VMEM((384, 128), BF16),
            pltpu.VMEM((2,) + chunk, BF16),
            pltpu.VMEM((2, CHUNKS, 4, CELLS, ROWS, 128), BF16),
            pltpu.VMEM((3, 5, 8, 128), F32),
            pltpu.VMEM((3, 4, 8, 128), F32),
            pltpu.VMEM((3, 5, 8, 128), F32),
            pltpu.VMEM((8, 128), F32),
            pltpu.VMEM((80, 128), F32),
            pltpu.VMEM(chunk, BF16),
            pltpu.VMEM(chunk, BF16),
            pltpu.VMEM(half, BF16),
            pltpu.VMEM(half, BF16),
            pltpu.VMEM((16, 16, 128), F32),
            pltpu.VMEM((16, 16, 128), F32),
            pltpu.VMEM((2, 8, 128), F32),
            pltpu.VMEM((4, 8, 128), F32),
            pltpu.VMEM((2, 4, 8, 128), F32),
            pltpu.VMEM((16, 8, 128), F32),
            dma((3,)),
            dma((4,)),
            dma((4,)),
            dma((2, CHUNKS, 4)),
            dma((2, CHUNKS, 4)),
            dma((3, 4)),
            dma((3, 4)),
            dma((3, 4)),
            dma((3, 4)),
            dma((CHUNKS,)),
            dma((CHUNKS,)),
            dma((CHUNKS,)),
            dma((CHUNKS,)),
            dma((CHUNKS,)),
            dma((CHUNKS,)),
            dma((16,)),
            dma((16,)),
            dma((4,)),
            dma((4,)),
            dma((2, 4)),
            dma((2, 4)),
            dma((16,)),
            dma((16,)),
        ],
        compiler_params=pltpu.CompilerParams(
            collective_id=0, has_side_effects=True, vmem_limit_bytes=48 * 1024 * 1024
        ),
        name="filter_and_gram",
    )(y0, potential, proj, energies, centers.T)
    filtered = out.reshape(6, 6, ORB, 128).transpose(2, 0, 1, 3)
    return filtered, gram


def solution(mesh):
    in_specs = (
        P("band", "sx", "sy", None),
        P("sx", "sy", None),
        P(("sx", "sy"), None, None, None),
        P(("sx", "sy"), None),
        P(("sx", "sy"), None),
    )
    out_specs = (P("band", "sx", "sy", None), P("band", None))
    return jax.shard_map(local, mesh=mesh, in_specs=in_specs, out_specs=out_specs, check_vma=False)
```

```python
import functools

import jax
import jax.numpy as jnp
from jax import lax
from jax.experimental import pallas as pl
from jax.experimental.pallas import tpu as pltpu
from jax.sharding import PartitionSpec as P

F32 = jnp.float32
BF16 = jnp.bfloat16
MESH = pl.DeviceIdType.MESH

stencil_weights = (
    -5369.0 / 1800.0,
    12.0 / 7.0,
    -15.0 / 56.0,
    10.0 / 189.0,
    -1.0 / 112.0,
    2.0 / 1925.0,
    -1.0 / 16632.0,
)
filter_center = 6.5
filter_half = 6.0

ORB = 64
CHUNKS = 4
ROWS = ORB // CHUNKS
CELLS = 36
HALF = CELLS // 2
PAIRS = 20
NEAR_ROWS = 24
GROUP = ORB // 2
NT = (((1,), (1,)), ((), ()))
NN = (((1,), (0,)), ((), ()))


def dot(a, b, dims=NN):
    return lax.dot_general(a, b, dims, preferred_element_type=F32)


def split(value):
    high = value.astype(BF16)
    return high, (value - high.astype(F32)).astype(BF16)


def kernel(
    cells_total,
    y0_hbm,
    pot_hbm,
    proj_hbm,
    energies,
    centers,
    out_hbm,
    gram,
    out,
    y0,
    pot,
    proj,
    y1,
    zn,
    msg,
    msg_in,
    weights,
    banded,
    sent,
    halo,
    part,
    part_in,
    coef,
    energy,
    wide,
    own,
    mate_in,
    far_in,
    cross_in,
    sums,
    scat_in,
    deep,
    deep_in,
    turn_in,
    whole,
    s_load,
    s_store,
    s_msg,
    r_msg,
    s_halo,
    r_halo,
    s_part,
    r_part,
    s_coef,
    r_coef,
    s_mate,
    r_mate,
    s_far,
    r_far,
    s_cross,
    r_cross,
    s_scat,
    r_scat,
    s_deep,
    r_deep,
    s_turn,
    r_turn,
    s_whole,
    r_whole,
):
    ix, iy, ib = lax.axis_index("sx"), lax.axis_index("sy"), lax.axis_index("band")
    group, core = ib // 2, lax.rem(ib, 2)
    row_y, low_z = iy // 4, lax.rem(iy, 4)
    plane = ix * 4 + row_y
    near = ({"sx": ix - 1}, {"sx": ix + 1}, {"sy": iy - 1}, {"sy": iy + 1})
    has = (ix > 0, ix < 3, iy > 0, iy < 15)
    mate = {"band": group * 2 + (1 - core)}
    far = {"band": (1 - group) * 2 + core}
    cross = {"band": (1 - group) * 2 + (1 - core)}

    def plane_peer(step):
        other = lax.rem(plane + step, 16)
        return other, {"sx": other // 4, "sy": lax.rem(other, 4) * 4 + low_z}

    def deep_peer(step):
        other = lax.rem(low_z + step, 4)
        return other, {"sy": row_y * 4 + other}

    def remote(src, dst, send, recv, device):
        return pltpu.make_async_remote_copy(
            src_ref=src,
            dst_ref=dst,
            send_sem=send,
            recv_sem=recv,
            device_id=device,
            device_id_type=MESH,
        )

    loads = [
        pltpu.make_async_copy(proj_hbm, proj, s_load.at[0]),
        pltpu.make_async_copy(y0_hbm, y0, s_load.at[1]),
        pltpu.make_async_copy(pot_hbm, pot, s_load.at[2]),
    ]
    for load in loads:
        load.start()
    barrier = pltpu.get_barrier_semaphore()

    def greet(device):
        pl.semaphore_signal(barrier, inc=1, device_id=device, device_id_type=MESH)

    greet({"sx": lax.rem(ix + 1, 4)})
    greet({"sx": lax.rem(ix + 3, 4)})
    greet({"sy": lax.rem(iy + 1, 16)})
    greet({"sy": lax.rem(iy + 15, 16)})
    greet(mate)
    greet(far)
    greet(cross)

    @pl.loop(1, 16)
    def _(step):
        greet(plane_peer(step)[1])

    @pl.loop(1, 4)
    def _(step):
        device = deep_peer(step)[1]
        greet(device)
        greet({**device, **far})
        greet({**device, **cross})

    lane = lax.broadcasted_iota(jnp.int32, (8, 128), 1)
    line = lax.broadcasted_iota(jnp.int32, (8, 128), 0)
    atom = lane // 5
    tile = lane - atom * 5
    shift_x = jnp.where(tile == 1, -1, jnp.where(tile == 2, 1, 0))
    shift_y = jnp.where(tile == 3, -1, jnp.where(tile == 4, 1, 0))
    nowhere = jnp.full((8, 128), -1000, jnp.int32)
    cell_x, cell_y, near_x, near_y = nowhere, nowhere, nowhere, nowhere
    for a in range(4):
        cell_x = jnp.where(atom == a, centers[0, a], cell_x)
        cell_y = jnp.where(atom == a, centers[1, a], cell_y)
        near_x = jnp.where(lane == a, centers[0, a], near_x)
        near_y = jnp.where(lane == a, centers[1, a], near_y)
    own_cells = jnp.where(line == 0, cell_x + shift_x, cell_y + shift_y).astype(F32)
    loads[0].wait()
    for s, (step_x, step_y) in enumerate(((-1, 0), (1, 0), (0, -1), (0, 1))):
        shifted = jnp.where(line == 0, near_x + step_x, near_y + step_y)
        msg[s, 16:24, :] = shifted.astype(F32)
        for p in range(4):
            msg[s, 4 * p : 4 * p + 4, :] = proj[:, s + 1, p, :]
    for s in range(4):

        @pl.when(jnp.logical_not(has[s]))
        def _(s=s):
            msg_in[s, 0:16] = jnp.zeros((16, 128), F32)
            msg_in[s, 16:24] = jnp.full((8, 128), -1000.0, F32)
            for phase in range(2):

                @pl.loop(0, CHUNKS)
                def _(c, phase=phase):
                    halo[phase, c, s] = jnp.zeros((CELLS, ROWS, 128), BF16)

            @pl.loop(0, 3)
            def _(k):
                part_in[k, s] = jnp.zeros((8, 128), F32)
                coef[k, 1 + s] = jnp.zeros((8, 128), F32)

    wide[...] = jnp.zeros((80, 128), F32)

    distance = jnp.abs(
        lax.broadcasted_iota(jnp.int32, (128, 128), 0)
        - lax.broadcasted_iota(jnp.int32, (128, 128), 1)
    )
    band = jnp.zeros((128, 128), F32)
    for step in range(1, 7):
        band = jnp.where(distance == step, -0.5 * stencil_weights[step], band)
    band_high, band_low = split(band)
    banded[0:128, :] = band_high
    banded[128:256, :] = band_high
    banded[256:384, :] = band_low

    level = jnp.zeros((8, 128), F32)
    for p in range(4):
        for a in range(4):
            row = 4 * p + a
            here = (line == row % 8) & ((lane >= 64) == (row >= 8))
            level = jnp.where(here, energies[a, p], level)
    energy[...] = level

    def rows_of(c):
        return pl.ds(pl.multiple_of(c * ROWS, ROWS), ROWS)

    loads[1].wait()
    @pl.loop(0, CHUNKS)
    def _(c):
        sent[0, c] = y0[:, rows_of(c), :].astype(BF16)


    pl.semaphore_wait(barrier, 7 + 15 + 9)

    def msg_copy(s):
        return remote(msg.at[s], msg_in.at[s ^ 1], s_msg.at[s], r_msg.at[s ^ 1], near[s])

    def halo_copy(phase, c, s):
        return remote(
            sent.at[phase, c],
            halo.at[phase, c, s ^ 1],
            s_halo.at[phase, c, s],
            r_halo.at[phase, c, s ^ 1],
            near[s],
        )

    def part_copy(k, s):
        return remote(
            part.at[k, 1 + s], part_in.at[k, s ^ 1], s_part.at[k, s], r_part.at[k, s ^ 1], near[s]
        )

    def coef_copy(k, s):
        return remote(
            coef.at[k, 0], coef.at[k, 1 + (s ^ 1)], s_coef.at[k, s], r_coef.at[k, s ^ 1], near[s]
        )

    def start_all(copy, *index):
        for s in range(4):

            @pl.when(has[s])
            def _(s=s):
                copy(*index, s).start()

    def arrive_all(copy, *index):
        for s in range(4):

            @pl.when(has[s])
            def _(s=s):
                copy(*index, s ^ 1).wait_recv()

    def sent_all(copy, *index):
        for s in range(4):

            @pl.when(has[s])
            def _(s=s):
                copy(*index, s).wait_send()

    start_all(msg_copy)
    start_all(halo_copy, 0, 0)

    arrive_all(msg_copy)
    first_x, first_y = (ix * 6).astype(F32), (iy * 6).astype(F32)
    def placed_rows(coords, which, count):
        local_x, local_y = coords[0:1] - first_x, coords[1:2] - first_y
        inside = (local_x >= 0) & (local_x < 6) & (local_y >= 0) & (local_y < 6)
        inside = inside & (lane[0:1] < count)
        place = jnp.where(inside, (local_x * 6 + local_y) * 80 + which, -1000.0)
        return jnp.broadcast_to(place, (8, 128))

    key = placed_rows(own_cells, atom[0:1].astype(F32), PAIRS)
    for s in range(4):
        start = PAIRS + 4 * s
        which = lane[0:1].astype(F32) + 16.0 * (s + 1)
        moved = pltpu.roll(placed_rows(msg_in[s, 16:24, :], which, 4), start, 1)
        key = jnp.where((lane >= start) & (lane < start + 4), moved, key)
    key = jnp.where(lane < 64, key, pltpu.roll(key, 64, 1) + 4.0)[0:1]
    tables = []
    for p in range(4):
        stacked = [proj[a, :, p, :] for a in range(4)]
        stacked += [msg_in[s, 4 * p : 4 * p + 4, :] for s in range(4)]
        table = jnp.concatenate(stacked + [jnp.zeros((28, 128), F32)], axis=0)
        tables.append(jnp.concatenate(split(table), axis=1))
    table = jnp.concatenate(tables, axis=0)

    @pl.loop(0, 9, unroll=3)
    def _(block):
        row = lax.broadcasted_iota(jnp.int32, (320, 128), 0) + block * 320
        row = row.astype(F32)
        masks = [jnp.where(row == key + 8.0 * p, 1.0, 0.0).astype(BF16) for p in range(2)]
        placed = dot(jnp.concatenate(masks, axis=1), table)
        placed = placed.reshape(4, 80, 256).astype(BF16)
        weights[pl.ds(block * 4, 4), 0:80, :] = placed[:, :, :128]
        weights[pl.ds(block * 4, 4), 80:160, :] = placed[:, :, :128]
        weights[pl.ds(block * 4, 4), 160:240, :] = placed[:, :, 128:]

    def partial(k, count, source):
        def step(cell, total):
            high, low = split(source(cell))
            w_high, w_low = weights[cell, 0:80, :], weights[cell, 160:240, :]
            left = jnp.concatenate([w_high, w_low, w_high], axis=1)
            right = jnp.concatenate([high, high, low], axis=1)
            return total + dot(left, right, NT)

        total = lax.fori_loop(0, CELLS, step, jnp.zeros((80, count), F32), unroll=12)
        wide[:, 0:count] = total
        for s in range(5):
            upper = pltpu.roll(wide[16 * s + 8 : 16 * s + 16, :], 64, 1)
            part[k, s] = jnp.where(lane < 64, wide[16 * s : 16 * s + 8, :], upper)
        start_all(part_copy, k)

    def finish_coef(k):
        arrive_all(part_copy, k)
        total = part[k, 0]
        for s in range(4):
            total = total + part_in[k, s]
        coef[k, 0] = total * energy[...]
        start_all(coef_copy, k)

    def along_z(rows, count, source):
        for x in range(6):
            high, low = split(source(x).reshape(6 * count, 128))
            left = jnp.concatenate([high, low, high], axis=1)
            zn[6 * x : 6 * x + 6, rows] = dot(left, banded[...]).reshape(6, count, 128)

    def projected(k, rows, count):
        arrive_all(coef_copy, k)
        parts = []
        for s in range(5):
            parts += [coef[k, s], pltpu.roll(coef[k, s], 64, 1)]
        stacked = jnp.concatenate(parts, axis=0)
        high = stacked.astype(BF16).astype(F32)
        low = (stacked - high).astype(BF16).astype(F32)
        left = jnp.concatenate([high, low, high], axis=0).T[0:count, :].astype(BF16)

        @pl.loop(0, CELLS, unroll=12)
        def _(cell):
            zn[cell, rows] += dot(left, weights[cell])

    center = -1.5 * stencil_weights[0] - filter_center

    def stencil(phase, c, source, finish):
        for x in range(6):

            def layer(other):
                if other < 0:
                    return halo[phase, c, 0, 6 * (other + 6) : 6 * (other + 7)].astype(F32)
                if other > 5:
                    return halo[phase, c, 1, 6 * (other - 6) : 6 * (other - 5)].astype(F32)
                return source(other)

            here = source(x)
            line_y = jnp.concatenate(
                [
                    halo[phase, c, 2, 6 * x : 6 * x + 6].astype(F32),
                    here,
                    halo[phase, c, 3, 6 * x : 6 * x + 6].astype(F32),
                ],
                axis=0,
            )
            total = zn[6 * x : 6 * x + 6, rows_of(c), :]
            total = total + here * (pot[x][:, None, :] + center)
            for step in range(1, 7):
                weight = -0.5 * stencil_weights[step]
                pair = layer(x - step) + layer(x + step)
                pair = pair + line_y[6 - step : 12 - step] + line_y[6 + step : 12 + step]
                total = total + weight * pair
            finish(x, total)

    everyone = pl.ds(0, ORB)
    partial(0, ORB, lambda cell: y0[cell])
    start_all(halo_copy, 0, 1)
    finish_coef(0)
    start_all(halo_copy, 0, 2)
    start_all(halo_copy, 0, 3)
    along_z(everyone, ORB, lambda x: y0[6 * x : 6 * x + 6])
    loads[2].wait()
    projected(0, everyone, ORB)

    def group_rows(g):
        return pl.ds(pl.multiple_of(g * GROUP, GROUP), GROUP)

    @pl.loop(0, 2)
    def _(g):
        @pl.loop(2 * g, 2 * g + 2)
        def _(c):
            arrive_all(halo_copy, 0, c)

            def finish(x, total):
                value = total * (1.0 / filter_half)
                y1[6 * x : 6 * x + 6, rows_of(c), :] = value
                sent[1, c, 6 * x : 6 * x + 6] = value.astype(BF16)

            stencil(0, c, lambda x: y0[6 * x : 6 * x + 6, rows_of(c), :], finish)

        partial(1 + g, GROUP, lambda cell: y1[cell, group_rows(g), :])
        start_all(halo_copy, 1, g)

    finish_coef(1)
    finish_coef(2)
    start_all(halo_copy, 1, 2)
    start_all(halo_copy, 1, 3)

    def store_copy(c):
        return pltpu.make_async_copy(
            out.at[:, rows_of(c), :], out_hbm.at[:, rows_of(c), :], s_store.at[c]
        )

    def mate_copy(c):
        return remote(own.at[c], mate_in.at[c], s_mate.at[c], r_mate.at[c], mate)

    def far_copy(c):
        start = pl.multiple_of(group * HALF, HALF)
        return remote(
            own.at[c, pl.ds(start, HALF)], far_in.at[c], s_far.at[c], r_far.at[c], far
        )

    def cross_copy(c):
        return remote(far_in.at[c], cross_in.at[c], s_cross.at[c], r_cross.at[c], mate)

    @pl.loop(0, 2)
    def _(g):
        along_z(group_rows(g), GROUP, lambda x: y1[6 * x : 6 * x + 6, group_rows(g), :])
        projected(1 + g, group_rows(g), GROUP)

        @pl.loop(2 * g, 2 * g + 2)
        def _(c):
            arrive_all(halo_copy, 1, c)

            def finish(x, total):
                before = y0[6 * x : 6 * x + 6, rows_of(c), :]
                value = total * (2.0 / filter_half) - before
                out[6 * x : 6 * x + 6, rows_of(c), :] = value
                own[c, 6 * x : 6 * x + 6] = value.astype(BF16)

            stencil(1, c, lambda x: y1[6 * x : 6 * x + 6, rows_of(c), :], finish)
            far_copy(c).start()
            mate_copy(c).start()
            store_copy(c).start()

    @pl.loop(0, CHUNKS)
    def _(c):
        mate_copy(c).wait_recv()

    def gather(ref, cell):
        return jnp.concatenate([ref[c, cell] for c in range(CHUNKS)], axis=0)

    def in_order(first, second):
        return jnp.concatenate(
            [jnp.where(core == 0, first, second), jnp.where(core == 0, second, first)], axis=0
        )

    def near_step(cell, total):
        mine = gather(own, cell)
        return total + dot(mine, in_order(mine, gather(mate_in, cell)), NT)

    near_sum = lax.fori_loop(0, CELLS, near_step, jnp.zeros((ORB, 128), F32), unroll=12)
    sums[:, 0:4] = near_sum.reshape(16, 4, 128)

    @pl.loop(0, CHUNKS)
    def _(c):
        far_copy(c).wait_recv()
        cross_copy(c).start()

    @pl.loop(0, CHUNKS)
    def _(c):
        cross_copy(c).wait_recv()

    def far_step(cell, totals):
        mine = gather(own, (1 - group) * HALF + cell)
        theirs, others = gather(far_in, cell), gather(cross_in, cell)
        straight = totals[0] + dot(mine, in_order(theirs, others), NT)
        both = jnp.concatenate([theirs, others], axis=0)
        zero = jnp.zeros_like(mine)
        turned = totals[1] + dot(both, in_order(mine, zero), NT)
        return straight, turned

    start = (jnp.zeros((ORB, 128), F32), jnp.zeros((2 * ORB, 128), F32))
    far_sum, turned = lax.fori_loop(0, HALF, far_step, start, unroll=9)

    sums[:, 4:8] = far_sum.reshape(16, 4, 128)
    sums[:, 8:12] = turned[:ORB].reshape(16, 4, 128)
    sums[:, 12:16] = turned[ORB:].reshape(16, 4, 128)

    def scat_copy(step):
        other, device = plane_peer(step)
        return remote(
            sums.at[other], scat_in.at[step], s_scat.at[step], r_scat.at[step], device
        )

    def whole_copy(step):
        device = plane_peer(step)[1]
        return remote(
            whole.at[plane], whole.at[plane], s_whole.at[step], r_whole.at[step], device
        )

    def deep_copy(step):
        device = deep_peer(step)[1]
        return remote(deep.at[0], deep_in.at[step], s_deep.at[step], r_deep.at[step], device)

    def turn_copy(side, step):
        device = {**deep_peer(step)[1], **(far, cross)[side]}
        return remote(
            deep.at[1],
            turn_in.at[side, step],
            s_turn.at[side, step],
            r_turn.at[side, step],
            device,
        )

    @pl.loop(1, 16)
    def _(step):
        scat_copy(step).start()

    def add_scat(step, total):
        scat_copy(step).wait_recv()
        return total + scat_in[step]

    mine = lax.fori_loop(1, 16, add_scat, sums[plane])
    deep[0] = mine[0:8]
    deep[1] = mine[8:16]
    for step in range(4):
        for side in range(2):
            turn_copy(side, step).start()
    for step in range(1, 4):
        deep_copy(step).start()
    mine = mine[0:8]
    for step in range(1, 4):
        deep_copy(step).wait_recv()
        mine = mine + deep_in[step]
    turned_in = jnp.zeros((4, 128), F32)
    for step in range(4):
        for side in range(2):
            turn_copy(side, step).wait_recv()
            turned_in = turned_in + turn_in[side, step, 4 * side : 4 * side + 4]
    mine = mine + jnp.concatenate([jnp.zeros((4, 128), F32), turned_in], axis=0)
    whole[plane] = mine * (1.0 / cells_total)

    @pl.loop(1, 16)
    def _(step):
        whole_copy(step).start()

    @pl.loop(1, 16)
    def _(step):
        other = lax.rem(plane + 16 - step, 16)
        remote(
            whole.at[other],
            whole.at[other],
            s_whole.at[step],
            r_whole.at[step],
            plane_peer(step)[1],
        ).wait_recv()

    near_all = whole[:, 0:4].reshape(ORB, 128)
    far_all = whole[:, 4:8].reshape(ORB, 128)
    gram[:, 0:128] = jnp.where(group == 0, near_all, far_all)
    gram[:, 128:256] = jnp.where(group == 0, far_all, near_all)

    sent_all(msg_copy)
    for phase in range(2):

        @pl.loop(0, CHUNKS)
        def _(c, phase=phase):
            sent_all(halo_copy, phase, c)

    @pl.loop(0, 3)
    def _(k):
        sent_all(part_copy, k)
        sent_all(coef_copy, k)

    @pl.loop(0, CHUNKS)
    def _(c):
        store_copy(c).wait()
        mate_copy(c).wait_send()
        far_copy(c).wait_send()
        cross_copy(c).wait_send()

    @pl.loop(1, 16)
    def _(step):
        scat_copy(step).wait_send()
        whole_copy(step).wait_send()

    for step in range(4):
        for side in range(2):
            turn_copy(side, step).wait_send()
    for step in range(1, 4):
        deep_copy(step).wait_send()


def local(orbitals, potential, projectors, energies, centers):
    y0 = orbitals.transpose(1, 2, 0, 3).reshape(CELLS, ORB, 128)
    proj = projectors.transpose(0, 2, 1, 3)
    cells_total = CELLS * 128 * lax.axis_size("sx") * lax.axis_size("sy")
    vmem = pl.BlockSpec(memory_space=pltpu.VMEM)
    anywhere = pl.BlockSpec(memory_space=pl.ANY)
    smem = pl.BlockSpec(memory_space=pltpu.SMEM)
    dma = pltpu.SemaphoreType.DMA
    chunk = (CHUNKS, CELLS, ROWS, 128)
    half = (CHUNKS, HALF, ROWS, 128)
    out, gram = pl.pallas_call(
        functools.partial(kernel, cells_total),
        out_shape=(
            jax.ShapeDtypeStruct((CELLS, ORB, 128), F32),
            jax.ShapeDtypeStruct((ORB, 256), F32),
        ),
        in_specs=[anywhere, anywhere, anywhere, smem, smem],
        out_specs=(anywhere, vmem),
        scratch_shapes=[
            pltpu.VMEM((CELLS, ORB, 128), F32),
            pltpu.VMEM((CELLS, ORB, 128), F32),
            pltpu.VMEM((6, 6, 128), F32),
            pltpu.VMEM((4, 5, 4, 128), F32),
            pltpu.VMEM((CELLS, ORB, 128), F32),
            pltpu.VMEM((CELLS, ORB, 128), F32),
            pltpu.VMEM((4, NEAR_ROWS, 128), F32),
            pltpu.VMEM((4, NEAR_ROWS, 128), F32),
            pltpu.VMEM((CELLS, 240, 128), BF16),
            pltpu.VMEM((384, 128), BF16),
            pltpu.VMEM((2,) + chunk, BF16),
            pltpu.VMEM((2, CHUNKS, 4, CELLS, ROWS, 128), BF16),
            pltpu.VMEM((3, 5, 8, 128), F32),
            pltpu.VMEM((3, 4, 8, 128), F32),
            pltpu.VMEM((3, 5, 8, 128), F32),
            pltpu.VMEM((8, 128), F32),
            pltpu.VMEM((80, 128), F32),
            pltpu.VMEM(chunk, BF16),
            pltpu.VMEM(chunk, BF16),
            pltpu.VMEM(half, BF16),
            pltpu.VMEM(half, BF16),
            pltpu.VMEM((16, 16, 128), F32),
            pltpu.VMEM((16, 16, 128), F32),
            pltpu.VMEM((2, 8, 128), F32),
            pltpu.VMEM((4, 8, 128), F32),
            pltpu.VMEM((2, 4, 8, 128), F32),
            pltpu.VMEM((16, 8, 128), F32),
            dma((3,)),
            dma((CHUNKS,)),
            dma((4,)),
            dma((4,)),
            dma((2, CHUNKS, 4)),
            dma((2, CHUNKS, 4)),
            dma((3, 4)),
            dma((3, 4)),
            dma((3, 4)),
            dma((3, 4)),
            dma((CHUNKS,)),
            dma((CHUNKS,)),
            dma((CHUNKS,)),
            dma((CHUNKS,)),
            dma((CHUNKS,)),
            dma((CHUNKS,)),
            dma((16,)),
            dma((16,)),
            dma((4,)),
            dma((4,)),
            dma((2, 4)),
            dma((2, 4)),
            dma((16,)),
            dma((16,)),
        ],
        compiler_params=pltpu.CompilerParams(
            collective_id=0, has_side_effects=True, vmem_limit_bytes=60 * 1024 * 1024
        ),
        name="filter_and_gram",
    )(y0, potential, proj, energies, centers.T)
    filtered = out.reshape(6, 6, ORB, 128).transpose(2, 0, 1, 3)
    return filtered, gram


def solution(mesh):
    in_specs = (
        P("band", "sx", "sy", None),
        P("sx", "sy", None),
        P(("sx", "sy"), None, None, None),
        P(("sx", "sy"), None),
        P(("sx", "sy"), None),
    )
    out_specs = (P("band", "sx", "sy", None), P("band", None))
    return jax.shard_map(local, mesh=mesh, in_specs=in_specs, out_specs=out_specs, check_vma=False)
```

```python
import functools

import jax
import jax.numpy as jnp
from jax import lax
from jax.experimental import pallas as pl
from jax.experimental.pallas import tpu as pltpu
from jax.sharding import PartitionSpec as P

F32 = jnp.float32
BF16 = jnp.bfloat16
MESH = pl.DeviceIdType.MESH

stencil_weights = (
    -5369.0 / 1800.0,
    12.0 / 7.0,
    -15.0 / 56.0,
    10.0 / 189.0,
    -1.0 / 112.0,
    2.0 / 1925.0,
    -1.0 / 16632.0,
)
filter_center = 6.5
filter_half = 6.0

ORB = 64
CHUNKS = 4
ROWS = ORB // CHUNKS
CELLS = 36
HALF = CELLS // 2
PAIRS = 20
NEAR_ROWS = 24
GROUP = ORB // 2
NT = (((1,), (1,)), ((), ()))
NN = (((1,), (0,)), ((), ()))


def dot(a, b, dims=NN):
    return lax.dot_general(a, b, dims, preferred_element_type=F32)


def split(value):
    high = value.astype(BF16)
    return high, (value - high.astype(F32)).astype(BF16)


def kernel(
    cells_total,
    y0_hbm,
    pot_hbm,
    proj_hbm,
    energies,
    centers,
    out_hbm,
    gram,
    out,
    y0,
    pot,
    proj,
    y1,
    zn,
    msg,
    msg_in,
    weights,
    banded,
    sent,
    halo,
    part,
    part_in,
    coef,
    energy,
    wide,
    own,
    mate_in,
    far_in,
    cross_in,
    sums,
    scat_in,
    deep,
    deep_in,
    turn_in,
    whole,
    s_load,
    s_store,
    s_msg,
    r_msg,
    s_halo,
    r_halo,
    s_part,
    r_part,
    s_coef,
    r_coef,
    s_mate,
    r_mate,
    s_far,
    r_far,
    s_cross,
    r_cross,
    s_scat,
    r_scat,
    s_deep,
    r_deep,
    s_turn,
    r_turn,
    s_whole,
    r_whole,
):
    ix, iy, ib = lax.axis_index("sx"), lax.axis_index("sy"), lax.axis_index("band")
    group, core = ib // 2, lax.rem(ib, 2)
    row_y, low_z = iy // 4, lax.rem(iy, 4)
    plane = ix * 4 + row_y
    near = ({"sx": ix - 1}, {"sx": ix + 1}, {"sy": iy - 1}, {"sy": iy + 1})
    has = (ix > 0, ix < 3, iy > 0, iy < 15)
    mate = {"band": group * 2 + (1 - core)}
    far = {"band": (1 - group) * 2 + core}
    cross = {"band": (1 - group) * 2 + (1 - core)}

    def plane_peer(step):
        other = lax.rem(plane + step, 16)
        return other, {"sx": other // 4, "sy": lax.rem(other, 4) * 4 + low_z}

    def deep_peer(step):
        other = lax.rem(low_z + step, 4)
        return other, {"sy": row_y * 4 + other}

    def remote(src, dst, send, recv, device):
        return pltpu.make_async_remote_copy(
            src_ref=src,
            dst_ref=dst,
            send_sem=send,
            recv_sem=recv,
            device_id=device,
            device_id_type=MESH,
        )

    loads = [
        pltpu.make_async_copy(proj_hbm, proj, s_load.at[0]),
        pltpu.make_async_copy(y0_hbm, y0, s_load.at[1]),
        pltpu.make_async_copy(pot_hbm, pot, s_load.at[2]),
    ]
    for load in loads:
        load.start()
    barrier = pltpu.get_barrier_semaphore()

    def greet(device):
        pl.semaphore_signal(barrier, inc=1, device_id=device, device_id_type=MESH)

    greet({"sx": lax.rem(ix + 1, 4)})
    greet({"sx": lax.rem(ix + 3, 4)})
    greet({"sy": lax.rem(iy + 1, 16)})
    greet({"sy": lax.rem(iy + 15, 16)})
    greet(mate)
    greet(far)
    greet(cross)

    @pl.loop(1, 16)
    def _(step):
        greet(plane_peer(step)[1])

    @pl.loop(1, 4)
    def _(step):
        device = deep_peer(step)[1]
        greet(device)
        greet({**device, **far})
        greet({**device, **cross})

    lane = lax.broadcasted_iota(jnp.int32, (8, 128), 1)
    line = lax.broadcasted_iota(jnp.int32, (8, 128), 0)
    atom = lane // 5
    tile = lane - atom * 5
    shift_x = jnp.where(tile == 1, -1, jnp.where(tile == 2, 1, 0))
    shift_y = jnp.where(tile == 3, -1, jnp.where(tile == 4, 1, 0))
    nowhere = jnp.full((8, 128), -1000, jnp.int32)
    cell_x, cell_y, near_x, near_y = nowhere, nowhere, nowhere, nowhere
    for a in range(4):
        cell_x = jnp.where(atom == a, centers[0, a], cell_x)
        cell_y = jnp.where(atom == a, centers[1, a], cell_y)
        near_x = jnp.where(lane == a, centers[0, a], near_x)
        near_y = jnp.where(lane == a, centers[1, a], near_y)
    own_cells = jnp.where(line == 0, cell_x + shift_x, cell_y + shift_y).astype(F32)
    loads[0].wait()
    for s, (step_x, step_y) in enumerate(((-1, 0), (1, 0), (0, -1), (0, 1))):
        shifted = jnp.where(line == 0, near_x + step_x, near_y + step_y)
        msg[s, 16:24, :] = shifted.astype(F32)
        for p in range(4):
            msg[s, 4 * p : 4 * p + 4, :] = proj[:, s + 1, p, :]
    for s in range(4):

        @pl.when(jnp.logical_not(has[s]))
        def _(s=s):
            msg_in[s, 0:16] = jnp.zeros((16, 128), F32)
            msg_in[s, 16:24] = jnp.full((8, 128), -1000.0, F32)
            for phase in range(2):

                @pl.loop(0, CHUNKS)
                def _(c, phase=phase):
                    halo[phase, c, s] = jnp.zeros((CELLS, ROWS, 128), BF16)

            @pl.loop(0, 3)
            def _(k):
                part_in[k, s] = jnp.zeros((8, 128), F32)
                coef[k, 1 + s] = jnp.zeros((8, 128), F32)

    wide[...] = jnp.zeros((80, 128), F32)

    distance = jnp.abs(
        lax.broadcasted_iota(jnp.int32, (128, 128), 0)
        - lax.broadcasted_iota(jnp.int32, (128, 128), 1)
    )
    band = jnp.zeros((128, 128), F32)
    for step in range(1, 7):
        band = jnp.where(distance == step, -0.5 * stencil_weights[step], band)
    band_high, band_low = split(band)
    banded[0:128, :] = band_high
    banded[128:256, :] = band_high
    banded[256:384, :] = band_low

    level = jnp.zeros((8, 128), F32)
    for p in range(4):
        for a in range(4):
            row = 4 * p + a
            here = (line == row % 8) & ((lane >= 64) == (row >= 8))
            level = jnp.where(here, energies[a, p], level)
    energy[...] = level

    def rows_of(c):
        return pl.ds(pl.multiple_of(c * ROWS, ROWS), ROWS)

    loads[1].wait()
    @pl.loop(0, CHUNKS)
    def _(c):
        sent[0, c] = y0[:, rows_of(c), :].astype(BF16)


    pl.semaphore_wait(barrier, 7 + 15 + 9)

    def msg_copy(s):
        return remote(msg.at[s], msg_in.at[s ^ 1], s_msg.at[s], r_msg.at[s ^ 1], near[s])

    def halo_copy(phase, c, s):
        return remote(
            sent.at[phase, c],
            halo.at[phase, c, s ^ 1],
            s_halo.at[phase, c, s],
            r_halo.at[phase, c, s ^ 1],
            near[s],
        )

    def part_copy(k, s):
        return remote(
            part.at[k, 1 + s], part_in.at[k, s ^ 1], s_part.at[k, s], r_part.at[k, s ^ 1], near[s]
        )

    def coef_copy(k, s):
        return remote(
            coef.at[k, 0], coef.at[k, 1 + (s ^ 1)], s_coef.at[k, s], r_coef.at[k, s ^ 1], near[s]
        )

    def start_all(copy, *index):
        for s in (2, 3, 0, 1):

            @pl.when(has[s])
            def _(s=s):
                copy(*index, s).start()

    def arrive_all(copy, *index):
        for s in range(4):

            @pl.when(has[s])
            def _(s=s):
                copy(*index, s ^ 1).wait_recv()

    def sent_all(copy, *index):
        for s in range(4):

            @pl.when(has[s])
            def _(s=s):
                copy(*index, s).wait_send()

    start_all(msg_copy)
    start_all(halo_copy, 0, 0)

    arrive_all(msg_copy)
    first_x, first_y = (ix * 6).astype(F32), (iy * 6).astype(F32)
    def placed_rows(coords, which, count):
        local_x, local_y = coords[0:1] - first_x, coords[1:2] - first_y
        inside = (local_x >= 0) & (local_x < 6) & (local_y >= 0) & (local_y < 6)
        inside = inside & (lane[0:1] < count)
        place = jnp.where(inside, (local_x * 6 + local_y) * 80 + which, -1000.0)
        return jnp.broadcast_to(place, (8, 128))

    key = placed_rows(own_cells, atom[0:1].astype(F32), PAIRS)
    for s in range(4):
        start = PAIRS + 4 * s
        which = lane[0:1].astype(F32) + 16.0 * (s + 1)
        moved = pltpu.roll(placed_rows(msg_in[s, 16:24, :], which, 4), start, 1)
        key = jnp.where((lane >= start) & (lane < start + 4), moved, key)
    key = jnp.where(lane < 64, key, pltpu.roll(key, 64, 1) + 4.0)[0:1]
    tables = []
    for p in range(4):
        stacked = [proj[a, :, p, :] for a in range(4)]
        stacked += [msg_in[s, 4 * p : 4 * p + 4, :] for s in range(4)]
        table = jnp.concatenate(stacked + [jnp.zeros((28, 128), F32)], axis=0)
        tables.append(jnp.concatenate(split(table), axis=1))
    table = jnp.concatenate(tables, axis=0)

    @pl.loop(0, 9, unroll=3)
    def _(block):
        row = lax.broadcasted_iota(jnp.int32, (320, 128), 0) + block * 320
        row = row.astype(F32)
        masks = [jnp.where(row == key + 8.0 * p, 1.0, 0.0).astype(BF16) for p in range(2)]
        placed = dot(jnp.concatenate(masks, axis=1), table)
        placed = placed.reshape(4, 80, 256).astype(BF16)
        weights[pl.ds(block * 4, 4), 0:80, :] = placed[:, :, :128]
        weights[pl.ds(block * 4, 4), 80:160, :] = placed[:, :, :128]
        weights[pl.ds(block * 4, 4), 160:240, :] = placed[:, :, 128:]

    def partial(k, count, source):
        def step(cell, total):
            high, low = split(source(cell))
            w_high, w_low = weights[cell, 0:80, :], weights[cell, 160:240, :]
            left = jnp.concatenate([w_high, w_low, w_high], axis=1)
            right = jnp.concatenate([high, high, low], axis=1)
            return total + dot(left, right, NT)

        total = lax.fori_loop(0, CELLS, step, jnp.zeros((80, count), F32), unroll=12)
        wide[:, 0:count] = total
        for s in range(5):
            upper = pltpu.roll(wide[16 * s + 8 : 16 * s + 16, :], 64, 1)
            part[k, s] = jnp.where(lane < 64, wide[16 * s : 16 * s + 8, :], upper)
        start_all(part_copy, k)

    def finish_coef(k):
        arrive_all(part_copy, k)
        total = part[k, 0]
        for s in range(4):
            total = total + part_in[k, s]
        coef[k, 0] = total * energy[...]
        start_all(coef_copy, k)

    def along_z(rows, count, source):
        for x in range(6):
            high, low = split(source(x).reshape(6 * count, 128))
            left = jnp.concatenate([high, low, high], axis=1)
            zn[6 * x : 6 * x + 6, rows] = dot(left, banded[...]).reshape(6, count, 128)

    def projected(k, rows, count):
        arrive_all(coef_copy, k)
        parts = []
        for s in range(5):
            parts += [coef[k, s], pltpu.roll(coef[k, s], 64, 1)]
        stacked = jnp.concatenate(parts, axis=0)
        high = stacked.astype(BF16).astype(F32)
        low = (stacked - high).astype(BF16).astype(F32)
        left = jnp.concatenate([high, low, high], axis=0).T[0:count, :].astype(BF16)

        @pl.loop(0, CELLS, unroll=12)
        def _(cell):
            zn[cell, rows] += dot(left, weights[cell])

    center = -1.5 * stencil_weights[0] - filter_center

    def stencil(phase, c, source, finish):
        for x in range(6):

            def layer(other):
                if other < 0:
                    return halo[phase, c, 0, 6 * (other + 6) : 6 * (other + 7)].astype(F32)
                if other > 5:
                    return halo[phase, c, 1, 6 * (other - 6) : 6 * (other - 5)].astype(F32)
                return source(other)

            here = source(x)
            line_y = jnp.concatenate(
                [
                    halo[phase, c, 2, 6 * x : 6 * x + 6].astype(F32),
                    here,
                    halo[phase, c, 3, 6 * x : 6 * x + 6].astype(F32),
                ],
                axis=0,
            )
            total = zn[6 * x : 6 * x + 6, rows_of(c), :]
            total = total + here * (pot[x][:, None, :] + center)
            for step in range(1, 7):
                weight = -0.5 * stencil_weights[step]
                pair = layer(x - step) + layer(x + step)
                pair = pair + line_y[6 - step : 12 - step] + line_y[6 + step : 12 + step]
                total = total + weight * pair
            finish(x, total)

    everyone = pl.ds(0, ORB)
    partial(0, ORB, lambda cell: y0[cell])
    start_all(halo_copy, 0, 1)
    finish_coef(0)
    start_all(halo_copy, 0, 2)
    start_all(halo_copy, 0, 3)
    along_z(everyone, ORB, lambda x: y0[6 * x : 6 * x + 6])
    loads[2].wait()
    projected(0, everyone, ORB)

    def group_rows(g):
        return pl.ds(pl.multiple_of(g * GROUP, GROUP), GROUP)

    @pl.loop(0, 2)
    def _(g):
        @pl.loop(2 * g, 2 * g + 2)
        def _(c):
            arrive_all(halo_copy, 0, c)

            def finish(x, total):
                value = total * (1.0 / filter_half)
                y1[6 * x : 6 * x + 6, rows_of(c), :] = value
                sent[1, c, 6 * x : 6 * x + 6] = value.astype(BF16)

            stencil(0, c, lambda x: y0[6 * x : 6 * x + 6, rows_of(c), :], finish)

        partial(1 + g, GROUP, lambda cell: y1[cell, group_rows(g), :])
        start_all(halo_copy, 1, g)

    finish_coef(1)
    finish_coef(2)
    start_all(halo_copy, 1, 2)
    start_all(halo_copy, 1, 3)

    def store_copy(c):
        return pltpu.make_async_copy(
            out.at[:, rows_of(c), :], out_hbm.at[:, rows_of(c), :], s_store.at[c]
        )

    def mate_copy(c):
        return remote(own.at[c], mate_in.at[c], s_mate.at[c], r_mate.at[c], mate)

    def far_copy(c):
        start = pl.multiple_of(group * HALF, HALF)
        return remote(
            own.at[c, pl.ds(start, HALF)], far_in.at[c], s_far.at[c], r_far.at[c], far
        )

    def cross_copy(c):
        return remote(far_in.at[c], cross_in.at[c], s_cross.at[c], r_cross.at[c], mate)

    @pl.loop(0, 2)
    def _(g):
        along_z(group_rows(g), GROUP, lambda x: y1[6 * x : 6 * x + 6, group_rows(g), :])
        projected(1 + g, group_rows(g), GROUP)

        @pl.loop(2 * g, 2 * g + 2)
        def _(c):
            arrive_all(halo_copy, 1, c)

            def finish(x, total):
                before = y0[6 * x : 6 * x + 6, rows_of(c), :]
                value = total * (2.0 / filter_half) - before
                out[6 * x : 6 * x + 6, rows_of(c), :] = value
                own[c, 6 * x : 6 * x + 6] = value.astype(BF16)

            stencil(1, c, lambda x: y1[6 * x : 6 * x + 6, rows_of(c), :], finish)
            far_copy(c).start()
            mate_copy(c).start()
            store_copy(c).start()

    @pl.loop(0, CHUNKS)
    def _(c):
        mate_copy(c).wait_recv()

    def gather(ref, cell):
        return jnp.concatenate([ref[c, cell] for c in range(CHUNKS)], axis=0)

    def in_order(first, second):
        return jnp.concatenate(
            [jnp.where(core == 0, first, second), jnp.where(core == 0, second, first)], axis=0
        )

    def near_step(cell, total):
        mine = gather(own, cell)
        return total + dot(mine, in_order(mine, gather(mate_in, cell)), NT)

    near_sum = lax.fori_loop(0, CELLS, near_step, jnp.zeros((ORB, 128), F32), unroll=12)
    sums[:, 0:4] = near_sum.reshape(16, 4, 128)

    @pl.loop(0, CHUNKS)
    def _(c):
        far_copy(c).wait_recv()
        cross_copy(c).start()

    @pl.loop(0, CHUNKS)
    def _(c):
        cross_copy(c).wait_recv()

    def far_step(cell, totals):
        mine = gather(own, (1 - group) * HALF + cell)
        theirs, others = gather(far_in, cell), gather(cross_in, cell)
        straight = totals[0] + dot(mine, in_order(theirs, others), NT)
        both = jnp.concatenate([theirs, others], axis=0)
        zero = jnp.zeros_like(mine)
        turned = totals[1] + dot(both, in_order(mine, zero), NT)
        return straight, turned

    start = (jnp.zeros((ORB, 128), F32), jnp.zeros((2 * ORB, 128), F32))
    far_sum, turned = lax.fori_loop(0, HALF, far_step, start, unroll=9)

    sums[:, 4:8] = far_sum.reshape(16, 4, 128)
    sums[:, 8:12] = turned[:ORB].reshape(16, 4, 128)
    sums[:, 12:16] = turned[ORB:].reshape(16, 4, 128)

    def scat_copy(step):
        other, device = plane_peer(step)
        return remote(
            sums.at[other], scat_in.at[step], s_scat.at[step], r_scat.at[step], device
        )

    def whole_copy(step):
        device = plane_peer(step)[1]
        return remote(
            whole.at[plane], whole.at[plane], s_whole.at[step], r_whole.at[step], device
        )

    def deep_copy(step):
        device = deep_peer(step)[1]
        return remote(deep.at[0], deep_in.at[step], s_deep.at[step], r_deep.at[step], device)

    def turn_copy(side, step):
        device = {**deep_peer(step)[1], **(far, cross)[side]}
        return remote(
            deep.at[1],
            turn_in.at[side, step],
            s_turn.at[side, step],
            r_turn.at[side, step],
            device,
        )

    @pl.loop(1, 16)
    def _(step):
        scat_copy(step).start()

    def add_scat(step, total):
        scat_copy(step).wait_recv()
        return total + scat_in[step]

    mine = lax.fori_loop(1, 16, add_scat, sums[plane])
    deep[0] = mine[0:8]
    deep[1] = mine[8:16]
    for step in range(4):
        for side in range(2):
            turn_copy(side, step).start()
    for step in range(1, 4):
        deep_copy(step).start()
    mine = mine[0:8]
    for step in range(1, 4):
        deep_copy(step).wait_recv()
        mine = mine + deep_in[step]
    turned_in = jnp.zeros((4, 128), F32)
    for step in range(4):
        for side in range(2):
            turn_copy(side, step).wait_recv()
            turned_in = turned_in + turn_in[side, step, 4 * side : 4 * side + 4]
    mine = mine + jnp.concatenate([jnp.zeros((4, 128), F32), turned_in], axis=0)
    whole[plane] = mine * (1.0 / cells_total)

    @pl.loop(1, 16)
    def _(step):
        whole_copy(step).start()

    @pl.loop(1, 16)
    def _(step):
        other = lax.rem(plane + 16 - step, 16)
        remote(
            whole.at[other],
            whole.at[other],
            s_whole.at[step],
            r_whole.at[step],
            plane_peer(step)[1],
        ).wait_recv()

    near_all = whole[:, 0:4].reshape(ORB, 128)
    far_all = whole[:, 4:8].reshape(ORB, 128)
    gram[:, 0:128] = jnp.where(group == 0, near_all, far_all)
    gram[:, 128:256] = jnp.where(group == 0, far_all, near_all)

    sent_all(msg_copy)
    for phase in range(2):

        @pl.loop(0, CHUNKS)
        def _(c, phase=phase):
            sent_all(halo_copy, phase, c)

    @pl.loop(0, 3)
    def _(k):
        sent_all(part_copy, k)
        sent_all(coef_copy, k)

    @pl.loop(0, CHUNKS)
    def _(c):
        store_copy(c).wait()
        mate_copy(c).wait_send()
        far_copy(c).wait_send()
        cross_copy(c).wait_send()

    @pl.loop(1, 16)
    def _(step):
        scat_copy(step).wait_send()
        whole_copy(step).wait_send()

    for step in range(4):
        for side in range(2):
            turn_copy(side, step).wait_send()
    for step in range(1, 4):
        deep_copy(step).wait_send()


def hand_on(out_from, gram_from, out_to, gram_to, out_here, gram_here, load_sem, store_sem):
    loads = [pltpu.make_async_copy(gram_from, gram_here, load_sem.at[CHUNKS])]
    stores = [pltpu.make_async_copy(gram_here, gram_to, store_sem.at[CHUNKS])]
    for c in range(CHUNKS):
        part = pl.ds(c * (CELLS // CHUNKS), CELLS // CHUNKS)
        loads.append(
            pltpu.make_async_copy(out_from.at[part], out_here.at[part], load_sem.at[c])
        )
        stores.append(
            pltpu.make_async_copy(out_here.at[part], out_to.at[part], store_sem.at[c])
        )
    for load in loads:
        load.start()
    for load, store in zip(loads, stores):
        load.wait()
        store.start()
    for store in stores:
        store.wait()


def local(orbitals, potential, projectors, energies, centers):
    y0 = orbitals.transpose(1, 2, 0, 3).reshape(CELLS, ORB, 128)
    proj = projectors.transpose(0, 2, 1, 3)
    cells_total = CELLS * 128 * lax.axis_size("sx") * lax.axis_size("sy")
    vmem = pl.BlockSpec(memory_space=pltpu.VMEM)
    anywhere = pl.BlockSpec(memory_space=pl.ANY)
    smem = pl.BlockSpec(memory_space=pltpu.SMEM)
    dma = pltpu.SemaphoreType.DMA
    chunk = (CHUNKS, CELLS, ROWS, 128)
    half = (CHUNKS, HALF, ROWS, 128)
    out, gram = pl.pallas_call(
        functools.partial(kernel, cells_total),
        out_shape=(
            jax.ShapeDtypeStruct((CELLS, ORB, 128), F32),
            jax.ShapeDtypeStruct((ORB, 256), F32),
        ),
        in_specs=[anywhere, anywhere, anywhere, smem, smem],
        out_specs=(anywhere, vmem),
        scratch_shapes=[
            pltpu.VMEM((CELLS, ORB, 128), F32),
            pltpu.VMEM((CELLS, ORB, 128), F32),
            pltpu.VMEM((6, 6, 128), F32),
            pltpu.VMEM((4, 5, 4, 128), F32),
            pltpu.VMEM((CELLS, ORB, 128), F32),
            pltpu.VMEM((CELLS, ORB, 128), F32),
            pltpu.VMEM((4, NEAR_ROWS, 128), F32),
            pltpu.VMEM((4, NEAR_ROWS, 128), F32),
            pltpu.VMEM((CELLS, 240, 128), BF16),
            pltpu.VMEM((384, 128), BF16),
            pltpu.VMEM((2,) + chunk, BF16),
            pltpu.VMEM((2, CHUNKS, 4, CELLS, ROWS, 128), BF16),
            pltpu.VMEM((3, 5, 8, 128), F32),
            pltpu.VMEM((3, 4, 8, 128), F32),
            pltpu.VMEM((3, 5, 8, 128), F32),
            pltpu.VMEM((8, 128), F32),
            pltpu.VMEM((80, 128), F32),
            pltpu.VMEM(chunk, BF16),
            pltpu.VMEM(chunk, BF16),
            pltpu.VMEM(half, BF16),
            pltpu.VMEM(half, BF16),
            pltpu.VMEM((16, 16, 128), F32),
            pltpu.VMEM((16, 16, 128), F32),
            pltpu.VMEM((2, 8, 128), F32),
            pltpu.VMEM((4, 8, 128), F32),
            pltpu.VMEM((2, 4, 8, 128), F32),
            pltpu.VMEM((16, 8, 128), F32),
            dma((3,)),
            dma((CHUNKS,)),
            dma((4,)),
            dma((4,)),
            dma((2, CHUNKS, 4)),
            dma((2, CHUNKS, 4)),
            dma((3, 4)),
            dma((3, 4)),
            dma((3, 4)),
            dma((3, 4)),
            dma((CHUNKS,)),
            dma((CHUNKS,)),
            dma((CHUNKS,)),
            dma((CHUNKS,)),
            dma((CHUNKS,)),
            dma((CHUNKS,)),
            dma((16,)),
            dma((16,)),
            dma((4,)),
            dma((4,)),
            dma((2, 4)),
            dma((2, 4)),
            dma((16,)),
            dma((16,)),
        ],
        compiler_params=pltpu.CompilerParams(
            collective_id=0, has_side_effects=True, vmem_limit_bytes=60 * 1024 * 1024
        ),
        name="filter_and_gram",
    )(y0, potential, proj, energies, centers.T)
    out, gram = pl.pallas_call(
        hand_on,
        out_shape=(
            jax.ShapeDtypeStruct((CELLS, ORB, 128), F32),
            jax.ShapeDtypeStruct((ORB, 256), F32),
        ),
        in_specs=[anywhere, anywhere],
        out_specs=(anywhere, anywhere),
        scratch_shapes=[
            pltpu.VMEM((CELLS, ORB, 128), F32),
            pltpu.VMEM((ORB, 256), F32),
            dma((CHUNKS + 1,)),
            dma((CHUNKS + 1,)),
        ],
        compiler_params=pltpu.CompilerParams(vmem_limit_bytes=60 * 1024 * 1024),
        name="hand_on",
    )(out, gram)
    filtered = out.reshape(6, 6, ORB, 128).transpose(2, 0, 1, 3)
    return filtered, gram


def solution(mesh):
    in_specs = (
        P("band", "sx", "sy", None),
        P("sx", "sy", None),
        P(("sx", "sy"), None, None, None),
        P(("sx", "sy"), None),
        P(("sx", "sy"), None),
    )
    out_specs = (P("band", "sx", "sy", None), P("band", None))
    return jax.shard_map(local, mesh=mesh, in_specs=in_specs, out_specs=out_specs, check_vma=False)
```

```python
import functools

import jax
import jax.numpy as jnp
from jax import lax
from jax.experimental import pallas as pl
from jax.experimental.pallas import tpu as pltpu
from jax.sharding import PartitionSpec as P

F32 = jnp.float32
BF16 = jnp.bfloat16
MESH = pl.DeviceIdType.MESH

stencil_weights = (
    -5369.0 / 1800.0,
    12.0 / 7.0,
    -15.0 / 56.0,
    10.0 / 189.0,
    -1.0 / 112.0,
    2.0 / 1925.0,
    -1.0 / 16632.0,
)
filter_center = 6.5
filter_half = 6.0

ORB = 64
CHUNKS = 4
ROWS = ORB // CHUNKS
CELLS = 36
HALF = CELLS // 2
PAIRS = 20
NEAR_ROWS = 24
GROUP = ORB // 2
NT = (((1,), (1,)), ((), ()))
NN = (((1,), (0,)), ((), ()))


def dot(a, b, dims=NN):
    return lax.dot_general(a, b, dims, preferred_element_type=F32)


def split(value):
    high = value.astype(BF16)
    return high, (value - high.astype(F32)).astype(BF16)


def kernel(
    cells_total,
    y0_hbm,
    pot_hbm,
    proj_hbm,
    energies,
    centers,
    out_hbm,
    gram,
    out,
    y0,
    pot,
    proj,
    y1,
    zn,
    msg,
    msg_in,
    weights,
    banded,
    sent,
    halo,
    part,
    part_in,
    coef,
    energy,
    wide,
    own,
    mate_in,
    far_in,
    cross_in,
    sums,
    scat_in,
    deep,
    deep_in,
    turn_in,
    whole,
    s_load,
    s_store,
    s_msg,
    r_msg,
    s_halo,
    r_halo,
    s_part,
    r_part,
    s_coef,
    r_coef,
    s_mate,
    r_mate,
    s_far,
    r_far,
    s_cross,
    r_cross,
    s_scat,
    r_scat,
    s_deep,
    r_deep,
    s_turn,
    r_turn,
    s_whole,
    r_whole,
):
    ix, iy, ib = lax.axis_index("sx"), lax.axis_index("sy"), lax.axis_index("band")
    group, core = ib // 2, lax.rem(ib, 2)
    row_y, low_z = iy // 4, lax.rem(iy, 4)
    plane = ix * 4 + row_y
    near = ({"sx": ix - 1}, {"sx": ix + 1}, {"sy": iy - 1}, {"sy": iy + 1})
    has = (ix > 0, ix < 3, iy > 0, iy < 15)
    mate = {"band": group * 2 + (1 - core)}
    far = {"band": (1 - group) * 2 + core}
    cross = {"band": (1 - group) * 2 + (1 - core)}

    def plane_peer(step):
        other = lax.rem(plane + step, 16)
        return other, {"sx": other // 4, "sy": lax.rem(other, 4) * 4 + low_z}

    def deep_peer(step):
        other = lax.rem(low_z + step, 4)
        return other, {"sy": row_y * 4 + other}

    def remote(src, dst, send, recv, device):
        return pltpu.make_async_remote_copy(
            src_ref=src,
            dst_ref=dst,
            send_sem=send,
            recv_sem=recv,
            device_id=device,
            device_id_type=MESH,
        )

    loads = [
        pltpu.make_async_copy(proj_hbm, proj, s_load.at[0]),
        pltpu.make_async_copy(y0_hbm, y0, s_load.at[1]),
        pltpu.make_async_copy(pot_hbm, pot, s_load.at[2]),
    ]
    for load in loads:
        load.start()
    barrier = pltpu.get_barrier_semaphore()

    def greet(device):
        pl.semaphore_signal(barrier, inc=1, device_id=device, device_id_type=MESH)

    greet({"sx": lax.rem(ix + 1, 4)})
    greet({"sx": lax.rem(ix + 3, 4)})
    greet({"sy": lax.rem(iy + 1, 16)})
    greet({"sy": lax.rem(iy + 15, 16)})
    greet(mate)
    greet(far)
    greet(cross)

    @pl.loop(1, 16)
    def _(step):
        greet(plane_peer(step)[1])

    @pl.loop(1, 4)
    def _(step):
        device = deep_peer(step)[1]
        greet(device)
        greet({**device, **far})
        greet({**device, **cross})

    lane = lax.broadcasted_iota(jnp.int32, (8, 128), 1)
    line = lax.broadcasted_iota(jnp.int32, (8, 128), 0)
    atom = lane // 5
    tile = lane - atom * 5
    shift_x = jnp.where(tile == 1, -1, jnp.where(tile == 2, 1, 0))
    shift_y = jnp.where(tile == 3, -1, jnp.where(tile == 4, 1, 0))
    nowhere = jnp.full((8, 128), -1000, jnp.int32)
    cell_x, cell_y, near_x, near_y = nowhere, nowhere, nowhere, nowhere
    for a in range(4):
        cell_x = jnp.where(atom == a, centers[0, a], cell_x)
        cell_y = jnp.where(atom == a, centers[1, a], cell_y)
        near_x = jnp.where(lane == a, centers[0, a], near_x)
        near_y = jnp.where(lane == a, centers[1, a], near_y)
    own_cells = jnp.where(line == 0, cell_x + shift_x, cell_y + shift_y).astype(F32)
    loads[0].wait()
    for s, (step_x, step_y) in enumerate(((-1, 0), (1, 0), (0, -1), (0, 1))):
        shifted = jnp.where(line == 0, near_x + step_x, near_y + step_y)
        msg[s, 16:24, :] = shifted.astype(F32)
        for p in range(4):
            msg[s, 4 * p : 4 * p + 4, :] = proj[:, s + 1, p, :]
    for s in range(4):

        @pl.when(jnp.logical_not(has[s]))
        def _(s=s):
            msg_in[s, 0:16] = jnp.zeros((16, 128), F32)
            msg_in[s, 16:24] = jnp.full((8, 128), -1000.0, F32)
            for phase in range(2):

                @pl.loop(0, CHUNKS)
                def _(c, phase=phase):
                    halo[phase, c, s] = jnp.zeros((CELLS, ROWS, 128), BF16)

            @pl.loop(0, 3)
            def _(k):
                part_in[k, s] = jnp.zeros((8, 128), F32)
                coef[k, 1 + s] = jnp.zeros((8, 128), F32)

    wide[...] = jnp.zeros((80, 128), F32)

    distance = jnp.abs(
        lax.broadcasted_iota(jnp.int32, (128, 128), 0)
        - lax.broadcasted_iota(jnp.int32, (128, 128), 1)
    )
    band = jnp.zeros((128, 128), F32)
    for step in range(1, 7):
        band = jnp.where(distance == step, -0.5 * stencil_weights[step], band)
    band_high, band_low = split(band)
    banded[0:128, :] = band_high
    banded[128:256, :] = band_high
    banded[256:384, :] = band_low

    level = jnp.zeros((8, 128), F32)
    for p in range(4):
        for a in range(4):
            row = 4 * p + a
            here = (line == row % 8) & ((lane >= 64) == (row >= 8))
            level = jnp.where(here, energies[a, p], level)
    energy[...] = level

    def rows_of(c):
        return pl.ds(pl.multiple_of(c * ROWS, ROWS), ROWS)

    loads[1].wait()
    @pl.loop(0, CHUNKS)
    def _(c):
        sent[0, c] = y0[:, rows_of(c), :].astype(BF16)


    pl.semaphore_wait(barrier, 7 + 15 + 9)

    def msg_copy(s):
        return remote(msg.at[s], msg_in.at[s ^ 1], s_msg.at[s], r_msg.at[s ^ 1], near[s])

    def halo_copy(phase, c, s):
        return remote(
            sent.at[phase, c],
            halo.at[phase, c, s ^ 1],
            s_halo.at[phase, c, s],
            r_halo.at[phase, c, s ^ 1],
            near[s],
        )

    def part_copy(k, s):
        return remote(
            part.at[k, 1 + s], part_in.at[k, s ^ 1], s_part.at[k, s], r_part.at[k, s ^ 1], near[s]
        )

    def coef_copy(k, s):
        return remote(
            coef.at[k, 0], coef.at[k, 1 + (s ^ 1)], s_coef.at[k, s], r_coef.at[k, s ^ 1], near[s]
        )

    def start_all(copy, *index, sides=(2, 3, 0, 1)):
        for s in sides:

            @pl.when(has[s])
            def _(s=s):
                copy(*index, s).start()

    def arrive_all(copy, *index):
        for s in range(4):

            @pl.when(has[s])
            def _(s=s):
                copy(*index, s ^ 1).wait_recv()

    def sent_all(copy, *index):
        for s in range(4):

            @pl.when(has[s])
            def _(s=s):
                copy(*index, s).wait_send()

    for sides in ((2, 3), (0, 1)):
        start_all(msg_copy, sides=sides)
        start_all(halo_copy, 0, 0, sides=sides)

    arrive_all(msg_copy)
    first_x, first_y = (ix * 6).astype(F32), (iy * 6).astype(F32)
    def placed_rows(coords, which, count):
        local_x, local_y = coords[0:1] - first_x, coords[1:2] - first_y
        inside = (local_x >= 0) & (local_x < 6) & (local_y >= 0) & (local_y < 6)
        inside = inside & (lane[0:1] < count)
        place = jnp.where(inside, (local_x * 6 + local_y) * 80 + which, -1000.0)
        return jnp.broadcast_to(place, (8, 128))

    key = placed_rows(own_cells, atom[0:1].astype(F32), PAIRS)
    for s in range(4):
        start = PAIRS + 4 * s
        which = lane[0:1].astype(F32) + 16.0 * (s + 1)
        moved = pltpu.roll(placed_rows(msg_in[s, 16:24, :], which, 4), start, 1)
        key = jnp.where((lane >= start) & (lane < start + 4), moved, key)
    key = jnp.where(lane < 64, key, pltpu.roll(key, 64, 1) + 4.0)[0:1]
    tables = []
    for p in range(4):
        stacked = [proj[a, :, p, :] for a in range(4)]
        stacked += [msg_in[s, 4 * p : 4 * p + 4, :] for s in range(4)]
        table = jnp.concatenate(stacked + [jnp.zeros((28, 128), F32)], axis=0)
        tables.append(jnp.concatenate(split(table), axis=1))
    table = jnp.concatenate(tables, axis=0)

    @pl.loop(0, 9, unroll=3)
    def _(block):
        row = lax.broadcasted_iota(jnp.int32, (320, 128), 0) + block * 320
        row = row.astype(F32)
        masks = [jnp.where(row == key + 8.0 * p, 1.0, 0.0).astype(BF16) for p in range(2)]
        placed = dot(jnp.concatenate(masks, axis=1), table)
        placed = placed.reshape(4, 80, 256).astype(BF16)
        weights[pl.ds(block * 4, 4), 0:80, :] = placed[:, :, :128]
        weights[pl.ds(block * 4, 4), 80:160, :] = placed[:, :, :128]
        weights[pl.ds(block * 4, 4), 160:240, :] = placed[:, :, 128:]

    def partial(k, count, source):
        def step(cell, total):
            high, low = split(source(cell))
            w_high, w_low = weights[cell, 0:80, :], weights[cell, 160:240, :]
            left = jnp.concatenate([w_high, w_low, w_high], axis=1)
            right = jnp.concatenate([high, high, low], axis=1)
            return total + dot(left, right, NT)

        total = lax.fori_loop(0, CELLS, step, jnp.zeros((80, count), F32), unroll=12)
        wide[:, 0:count] = total
        for s in range(5):
            upper = pltpu.roll(wide[16 * s + 8 : 16 * s + 16, :], 64, 1)
            part[k, s] = jnp.where(lane < 64, wide[16 * s : 16 * s + 8, :], upper)
        start_all(part_copy, k)

    def finish_coef(k):
        arrive_all(part_copy, k)
        total = part[k, 0]
        for s in range(4):
            total = total + part_in[k, s]
        coef[k, 0] = total * energy[...]
        start_all(coef_copy, k)

    def along_z(rows, count, source):
        for x in range(6):
            high, low = split(source(x).reshape(6 * count, 128))
            left = jnp.concatenate([high, low, high], axis=1)
            zn[6 * x : 6 * x + 6, rows] = dot(left, banded[...]).reshape(6, count, 128)

    def projected(k, rows, count):
        arrive_all(coef_copy, k)
        parts = []
        for s in range(5):
            parts += [coef[k, s], pltpu.roll(coef[k, s], 64, 1)]
        stacked = jnp.concatenate(parts, axis=0)
        high = stacked.astype(BF16).astype(F32)
        low = (stacked - high).astype(BF16).astype(F32)
        left = jnp.concatenate([high, low, high], axis=0).T[0:count, :].astype(BF16)

        @pl.loop(0, CELLS, unroll=12)
        def _(cell):
            zn[cell, rows] += dot(left, weights[cell])

    center = -1.5 * stencil_weights[0] - filter_center

    def stencil(phase, c, source, finish):
        for x in range(6):

            def layer(other):
                if other < 0:
                    return halo[phase, c, 0, 6 * (other + 6) : 6 * (other + 7)].astype(F32)
                if other > 5:
                    return halo[phase, c, 1, 6 * (other - 6) : 6 * (other - 5)].astype(F32)
                return source(other)

            here = source(x)
            line_y = jnp.concatenate(
                [
                    halo[phase, c, 2, 6 * x : 6 * x + 6].astype(F32),
                    here,
                    halo[phase, c, 3, 6 * x : 6 * x + 6].astype(F32),
                ],
                axis=0,
            )
            total = zn[6 * x : 6 * x + 6, rows_of(c), :]
            total = total + here * (pot[x][:, None, :] + center)
            for step in range(1, 7):
                weight = -0.5 * stencil_weights[step]
                pair = layer(x - step) + layer(x + step)
                pair = pair + line_y[6 - step : 12 - step] + line_y[6 + step : 12 + step]
                total = total + weight * pair
            finish(x, total)

    everyone = pl.ds(0, ORB)
    partial(0, ORB, lambda cell: y0[cell])
    start_all(halo_copy, 0, 1)
    finish_coef(0)
    start_all(halo_copy, 0, 2)
    start_all(halo_copy, 0, 3)
    along_z(everyone, ORB, lambda x: y0[6 * x : 6 * x + 6])
    loads[2].wait()
    projected(0, everyone, ORB)

    def group_rows(g):
        return pl.ds(pl.multiple_of(g * GROUP, GROUP), GROUP)

    @pl.loop(0, 2)
    def _(g):
        @pl.loop(2 * g, 2 * g + 2)
        def _(c):
            arrive_all(halo_copy, 0, c)

            def finish(x, total):
                value = total * (1.0 / filter_half)
                y1[6 * x : 6 * x + 6, rows_of(c), :] = value
                sent[1, c, 6 * x : 6 * x + 6] = value.astype(BF16)

            stencil(0, c, lambda x: y0[6 * x : 6 * x + 6, rows_of(c), :], finish)

        partial(1 + g, GROUP, lambda cell: y1[cell, group_rows(g), :])
        start_all(halo_copy, 1, g)

    finish_coef(1)
    finish_coef(2)
    start_all(halo_copy, 1, 2)
    start_all(halo_copy, 1, 3)

    def store_copy(c):
        return pltpu.make_async_copy(
            out.at[:, rows_of(c), :], out_hbm.at[:, rows_of(c), :], s_store.at[c]
        )

    def mate_copy(c):
        return remote(own.at[c], mate_in.at[c], s_mate.at[c], r_mate.at[c], mate)

    def far_copy(c):
        start = pl.multiple_of(group * HALF, HALF)
        return remote(
            own.at[c, pl.ds(start, HALF)], far_in.at[c], s_far.at[c], r_far.at[c], far
        )

    def cross_copy(c):
        return remote(far_in.at[c], cross_in.at[c], s_cross.at[c], r_cross.at[c], mate)

    @pl.loop(0, 2)
    def _(g):
        along_z(group_rows(g), GROUP, lambda x: y1[6 * x : 6 * x + 6, group_rows(g), :])
        projected(1 + g, group_rows(g), GROUP)

        @pl.loop(2 * g, 2 * g + 2)
        def _(c):
            arrive_all(halo_copy, 1, c)

            def finish(x, total):
                before = y0[6 * x : 6 * x + 6, rows_of(c), :]
                value = total * (2.0 / filter_half) - before
                out[6 * x : 6 * x + 6, rows_of(c), :] = value
                own[c, 6 * x : 6 * x + 6] = value.astype(BF16)

            stencil(1, c, lambda x: y1[6 * x : 6 * x + 6, rows_of(c), :], finish)
            far_copy(c).start()
            mate_copy(c).start()
            store_copy(c).start()

    @pl.loop(0, CHUNKS)
    def _(c):
        mate_copy(c).wait_recv()

    def gather(ref, cell):
        return jnp.concatenate([ref[c, cell] for c in range(CHUNKS)], axis=0)

    def in_order(first, second):
        return jnp.concatenate(
            [jnp.where(core == 0, first, second), jnp.where(core == 0, second, first)], axis=0
        )

    def near_step(cell, total):
        mine = gather(own, cell)
        return total + dot(mine, in_order(mine, gather(mate_in, cell)), NT)

    near_sum = lax.fori_loop(0, CELLS, near_step, jnp.zeros((ORB, 128), F32), unroll=12)
    sums[:, 0:4] = near_sum.reshape(16, 4, 128)

    @pl.loop(0, CHUNKS)
    def _(c):
        far_copy(c).wait_recv()
        cross_copy(c).start()

    @pl.loop(0, CHUNKS)
    def _(c):
        cross_copy(c).wait_recv()

    def far_step(cell, totals):
        mine = gather(own, (1 - group) * HALF + cell)
        theirs, others = gather(far_in, cell), gather(cross_in, cell)
        straight = totals[0] + dot(mine, in_order(theirs, others), NT)
        both = jnp.concatenate([theirs, others], axis=0)
        zero = jnp.zeros_like(mine)
        turned = totals[1] + dot(both, in_order(mine, zero), NT)
        return straight, turned

    start = (jnp.zeros((ORB, 128), F32), jnp.zeros((2 * ORB, 128), F32))
    far_sum, turned = lax.fori_loop(0, HALF, far_step, start, unroll=9)

    sums[:, 4:8] = far_sum.reshape(16, 4, 128)
    sums[:, 8:12] = turned[:ORB].reshape(16, 4, 128)
    sums[:, 12:16] = turned[ORB:].reshape(16, 4, 128)

    def scat_copy(step):
        other, device = plane_peer(step)
        return remote(
            sums.at[other], scat_in.at[step], s_scat.at[step], r_scat.at[step], device
        )

    def whole_copy(step):
        device = plane_peer(step)[1]
        return remote(
            whole.at[plane], whole.at[plane], s_whole.at[step], r_whole.at[step], device
        )

    def deep_copy(step):
        device = deep_peer(step)[1]
        return remote(deep.at[0], deep_in.at[step], s_deep.at[step], r_deep.at[step], device)

    def turn_copy(side, step):
        device = {**deep_peer(step)[1], **(far, cross)[side]}
        return remote(
            deep.at[1],
            turn_in.at[side, step],
            s_turn.at[side, step],
            r_turn.at[side, step],
            device,
        )

    @pl.loop(1, 16)
    def _(step):
        scat_copy(step).start()

    def add_scat(step, total):
        scat_copy(step).wait_recv()
        return total + scat_in[step]

    mine = lax.fori_loop(1, 16, add_scat, sums[plane])
    deep[0] = mine[0:8]
    deep[1] = mine[8:16]
    for step in range(4):
        for side in range(2):
            turn_copy(side, step).start()
    for step in range(1, 4):
        deep_copy(step).start()
    mine = mine[0:8]
    for step in range(1, 4):
        deep_copy(step).wait_recv()
        mine = mine + deep_in[step]
    turned_in = jnp.zeros((4, 128), F32)
    for step in range(4):
        for side in range(2):
            turn_copy(side, step).wait_recv()
            turned_in = turned_in + turn_in[side, step, 4 * side : 4 * side + 4]
    mine = mine + jnp.concatenate([jnp.zeros((4, 128), F32), turned_in], axis=0)
    whole[plane] = mine * (1.0 / cells_total)

    @pl.loop(1, 16)
    def _(step):
        whole_copy(step).start()

    @pl.loop(1, 16)
    def _(step):
        other = lax.rem(plane + 16 - step, 16)
        remote(
            whole.at[other],
            whole.at[other],
            s_whole.at[step],
            r_whole.at[step],
            plane_peer(step)[1],
        ).wait_recv()

    near_all = whole[:, 0:4].reshape(ORB, 128)
    far_all = whole[:, 4:8].reshape(ORB, 128)
    gram[:, 0:128] = jnp.where(group == 0, near_all, far_all)
    gram[:, 128:256] = jnp.where(group == 0, far_all, near_all)

    sent_all(msg_copy)
    for phase in range(2):

        @pl.loop(0, CHUNKS)
        def _(c, phase=phase):
            sent_all(halo_copy, phase, c)

    @pl.loop(0, 3)
    def _(k):
        sent_all(part_copy, k)
        sent_all(coef_copy, k)

    @pl.loop(0, CHUNKS)
    def _(c):
        store_copy(c).wait()
        mate_copy(c).wait_send()
        far_copy(c).wait_send()
        cross_copy(c).wait_send()

    @pl.loop(1, 16)
    def _(step):
        scat_copy(step).wait_send()
        whole_copy(step).wait_send()

    for step in range(4):
        for side in range(2):
            turn_copy(side, step).wait_send()
    for step in range(1, 4):
        deep_copy(step).wait_send()


def hand_on(out_from, gram_from, out_to, gram_to, out_here, gram_here, load_sem, store_sem):
    loads = [pltpu.make_async_copy(gram_from, gram_here, load_sem.at[CHUNKS])]
    stores = [pltpu.make_async_copy(gram_here, gram_to, store_sem.at[CHUNKS])]
    for c in range(CHUNKS):
        part = pl.ds(c * (CELLS // CHUNKS), CELLS // CHUNKS)
        loads.append(
            pltpu.make_async_copy(out_from.at[part], out_here.at[part], load_sem.at[c])
        )
        stores.append(
            pltpu.make_async_copy(out_here.at[part], out_to.at[part], store_sem.at[c])
        )
    for load in loads:
        load.start()
    for load, store in zip(loads, stores):
        load.wait()
        store.start()
    for store in stores:
        store.wait()


def local(orbitals, potential, projectors, energies, centers):
    y0 = orbitals.transpose(1, 2, 0, 3).reshape(CELLS, ORB, 128)
    proj = projectors.transpose(0, 2, 1, 3)
    cells_total = CELLS * 128 * lax.axis_size("sx") * lax.axis_size("sy")
    vmem = pl.BlockSpec(memory_space=pltpu.VMEM)
    anywhere = pl.BlockSpec(memory_space=pl.ANY)
    smem = pl.BlockSpec(memory_space=pltpu.SMEM)
    dma = pltpu.SemaphoreType.DMA
    chunk = (CHUNKS, CELLS, ROWS, 128)
    half = (CHUNKS, HALF, ROWS, 128)
    out, gram = pl.pallas_call(
        functools.partial(kernel, cells_total),
        out_shape=(
            jax.ShapeDtypeStruct((CELLS, ORB, 128), F32),
            jax.ShapeDtypeStruct((ORB, 256), F32),
        ),
        in_specs=[anywhere, anywhere, anywhere, smem, smem],
        out_specs=(anywhere, vmem),
        scratch_shapes=[
            pltpu.VMEM((CELLS, ORB, 128), F32),
            pltpu.VMEM((CELLS, ORB, 128), F32),
            pltpu.VMEM((6, 6, 128), F32),
            pltpu.VMEM((4, 5, 4, 128), F32),
            pltpu.VMEM((CELLS, ORB, 128), F32),
            pltpu.VMEM((CELLS, ORB, 128), F32),
            pltpu.VMEM((4, NEAR_ROWS, 128), F32),
            pltpu.VMEM((4, NEAR_ROWS, 128), F32),
            pltpu.VMEM((CELLS, 240, 128), BF16),
            pltpu.VMEM((384, 128), BF16),
            pltpu.VMEM((2,) + chunk, BF16),
            pltpu.VMEM((2, CHUNKS, 4, CELLS, ROWS, 128), BF16),
            pltpu.VMEM((3, 5, 8, 128), F32),
            pltpu.VMEM((3, 4, 8, 128), F32),
            pltpu.VMEM((3, 5, 8, 128), F32),
            pltpu.VMEM((8, 128), F32),
            pltpu.VMEM((80, 128), F32),
            pltpu.VMEM(chunk, BF16),
            pltpu.VMEM(chunk, BF16),
            pltpu.VMEM(half, BF16),
            pltpu.VMEM(half, BF16),
            pltpu.VMEM((16, 16, 128), F32),
            pltpu.VMEM((16, 16, 128), F32),
            pltpu.VMEM((2, 8, 128), F32),
            pltpu.VMEM((4, 8, 128), F32),
            pltpu.VMEM((2, 4, 8, 128), F32),
            pltpu.VMEM((16, 8, 128), F32),
            dma((3,)),
            dma((CHUNKS,)),
            dma((4,)),
            dma((4,)),
            dma((2, CHUNKS, 4)),
            dma((2, CHUNKS, 4)),
            dma((3, 4)),
            dma((3, 4)),
            dma((3, 4)),
            dma((3, 4)),
            dma((CHUNKS,)),
            dma((CHUNKS,)),
            dma((CHUNKS,)),
            dma((CHUNKS,)),
            dma((CHUNKS,)),
            dma((CHUNKS,)),
            dma((16,)),
            dma((16,)),
            dma((4,)),
            dma((4,)),
            dma((2, 4)),
            dma((2, 4)),
            dma((16,)),
            dma((16,)),
        ],
        compiler_params=pltpu.CompilerParams(
            collective_id=0, has_side_effects=True, vmem_limit_bytes=60 * 1024 * 1024
        ),
        name="filter_and_gram",
    )(y0, potential, proj, energies, centers.T)
    out, gram = pl.pallas_call(
        hand_on,
        out_shape=(
            jax.ShapeDtypeStruct((CELLS, ORB, 128), F32),
            jax.ShapeDtypeStruct((ORB, 256), F32),
        ),
        in_specs=[anywhere, anywhere],
        out_specs=(anywhere, anywhere),
        scratch_shapes=[
            pltpu.VMEM((CELLS, ORB, 128), F32),
            pltpu.VMEM((ORB, 256), F32),
            dma((CHUNKS + 1,)),
            dma((CHUNKS + 1,)),
        ],
        compiler_params=pltpu.CompilerParams(vmem_limit_bytes=60 * 1024 * 1024),
        name="hand_on",
    )(out, gram)
    filtered = out.reshape(6, 6, ORB, 128).transpose(2, 0, 1, 3)
    return filtered, gram


def solution(mesh):
    in_specs = (
        P("band", "sx", "sy", None),
        P("sx", "sy", None),
        P(("sx", "sy"), None, None, None),
        P(("sx", "sy"), None),
        P(("sx", "sy"), None),
    )
    out_specs = (P("band", "sx", "sy", None), P("band", None))
    return jax.shard_map(local, mesh=mesh, in_specs=in_specs, out_specs=out_specs, check_vma=False)
```
